32 devices in a mesh: row: 4 (over y, core), col: 8 (over z, x).
Axes of the slice: x: 2, y: 2, z: 4, core: 2. Of those that a mesh axis runs over, the one named last changes fastest.
Arguments:
- particles: float32 [1024, 128], P('row'), may hold values from -4 to 4
- log_weights: float32 [1024], P('row'), may hold values from -8 to 8
- targets: float32 [3072, 128], P('col'), may hold values from -5 to 5
Outputs:
- new_particles: float32 [3072, 128], P(('col', 'row'))
The draws below stay inside these ranges and needn't reach their ends.
All inputs are finite; a program needn't handle non-finite values.
Results may differ from the reference program's by a relative error of at most 0.005.
Values sent between devices are 32-bit elements; how exact they have to be, the bound alone decides.
A program may use at most 64 MiB of HBM per device.

```python
import math
import jax
import jax.numpy as jnp
from jax import lax

S = 128
ITERS = 3
N = 1024
M = 3072


def draw_particles(key, part):
    third = jax.random.fold_in(jax.random.fold_in(key, 11), 2)
    return jnp.clip(jax.random.normal(third, (N, S), jnp.float32), -4.0, 4.0)


def draw_targets(key, part):
    third = jax.random.fold_in(jax.random.fold_in(key, 23), 2)
    return jnp.clip(jax.random.normal(third, (M, S), jnp.float32), -5.0, 5.0)


def block_scale(rng, dims, shards, low, top_value):
    def one(position, parts):
        steps = jax.random.uniform(jax.random.fold_in(jax.random.fold_in(rng, 6), position), (parts,), jnp.float32, low / len(shards), top_value / len(shards))
        return jnp.repeat(jnp.exp(steps), dims[position] // parts).reshape((-1,) + (1,) * (len(dims) - position - 1))

    factor_of = one(*shards[0])
    for cut in shards[1:]:
        factor_of = factor_of * one(*cut)
    return factor_of


def centred(key, extent, deviation, limit, cuts=(), held_as=jnp.bfloat16):
    values = deviation * jax.random.normal(key, extent, jnp.float32)
    if cuts:
        values = values * block_scale(key, extent, cuts, -0.22, 0.18)
    return jnp.clip(values, -limit, limit).astype(held_as)


def setup_inputs(seed: int = 0) -> dict:
    key_list = jax.random.split(jax.random.key(seed), 4)
    return {
        "particles": draw_particles(jax.random.fold_in(key_list[3], 71), 0),
        "log_weights": centred(key_list[1], (N,), 2.0, 8.0, ((0, 4),), jnp.float32),
        "targets": draw_targets(jax.random.fold_in(key_list[3], 71), 0),
    }


EPS = 0.01


def cost_tile(source, points):
    source_sq = jnp.sum(source * source, axis=1)
    points_sq = jnp.sum(points * points, axis=1)
    cross = jnp.dot(source, points.T, precision=lax.Precision.HIGHEST, preferred_element_type=jnp.float32)
    return (source_sq[:, None] + points_sq[None, :] - 2.0 * cross) / source.shape[1]


def reference(particles, log_weights, targets):
    total = particles.shape[0]
    block_rows = math.gcd(total, 1024)
    block_count = total // block_rows
    stacked = particles.reshape(block_count, block_rows, particles.shape[1])
    weights_stacked = log_weights.reshape(block_count, block_rows)
    log_count = math.log(targets.shape[0])
    width = targets.shape[0]
    col_pot = jnp.zeros((width,), jnp.float32)
    col_lse = jnp.zeros((width,), jnp.float32)
    for iteration in range(ITERS):
        def row_fn(pair):
            source, weights = pair
            scores = (col_pot[None, :] - cost_tile(source, targets)) / EPS
            top = jnp.max(scores, axis=1)
            summed = jnp.sum(jnp.exp(scores - top[:, None]), axis=1)
            return EPS * (weights - (top + jnp.log(summed)))

        row_pot = lax.map(row_fn, (stacked, weights_stacked))

        def col_fn(carry, pair):
            top_old, sum_old = carry
            source, potential = pair
            scores = (potential[:, None] - cost_tile(source, targets)) / EPS
            top = jnp.maximum(top_old, jnp.max(scores, axis=0))
            summed = sum_old * jnp.exp(top_old - top) + jnp.sum(jnp.exp(scores - top[None, :]), axis=0)
            return (top, summed), None

        start = (jnp.full((width,), -1e30, jnp.float32), jnp.zeros((width,), jnp.float32))
        (top, summed), unused = lax.scan(col_fn, start, (stacked, row_pot))
        col_lse = top + jnp.log(summed)
        col_pot = EPS * (-log_count - col_lse)

    def move_fn(acc, pair):
        source, potential = pair
        plan = jnp.exp((potential[:, None] - cost_tile(source, targets)) / EPS - col_lse[None, :]).astype(jnp.bfloat16)
        moved = lax.dot_general(plan, source.astype(jnp.bfloat16), (((0,), (0,)), ((), ())), preferred_element_type=jnp.float32)
        return acc + moved, None

    result, unused = lax.scan(move_fn, jnp.zeros((width, particles.shape[1]), jnp.float32), (stacked, row_pot))
    return result
```

```python
import functools
import math

import jax
import jax.numpy as jnp
from jax import lax
from jax.experimental import pallas as pl
from jax.experimental.pallas import tpu as pltpu
from jax.sharding import PartitionSpec as P

ITERS = 3


EPS = 0.01
MESH = pl.DeviceIdType.MESH
HIGHEST = lax.Precision.HIGHEST
LANES = 128
CHUNK = 32
PIECES = 2


def cost_tile(source, points):
    source_sq = jnp.sum(source * source, axis=1)
    points_sq = jnp.sum(points * points, axis=1)
    cross = jnp.dot(source, points.T, precision=HIGHEST, preferred_element_type=jnp.float32)
    return (source_sq[:, None] + points_sq[None, :] - 2.0 * cross) / source.shape[1]


def row_update(particles, log_weights, targets, col_pot, block_count, block_rows):
    maxima = []
    totals = []
    for index in range(block_count):
        source = particles[index * block_rows : (index + 1) * block_rows]
        scores = (col_pot[None, :] - cost_tile(source, targets)) / EPS
        top = jnp.max(scores, axis=1)
        maxima.append(top)
        totals.append(jnp.sum(jnp.exp(scores - top[:, None]), axis=1))
    local_top = jnp.concatenate(maxima)
    local_sum = jnp.concatenate(totals)
    top = lax.pmax(local_top, "col")
    summed = lax.psum(local_sum * jnp.exp(local_top - top), "col")
    return EPS * (log_weights - (top + jnp.log(summed)))


def col_update(particles, targets, row_pot, block_count, block_rows):
    width = targets.shape[0]
    top = jnp.full((width,), -1e30, jnp.float32)
    summed = jnp.zeros((width,), jnp.float32)
    for index in range(block_count):
        source = particles[index * block_rows : (index + 1) * block_rows]
        potential = row_pot[index * block_rows : (index + 1) * block_rows]
        scores = (potential[:, None] - cost_tile(source, targets)) / EPS
        fresh = jnp.maximum(top, jnp.max(scores, axis=0))
        summed = summed * jnp.exp(top - fresh) + jnp.sum(jnp.exp(scores - fresh[None, :]), axis=0)
        top = fresh
    global_top = lax.pmax(top, "row")
    summed = lax.psum(summed * jnp.exp(top - global_top), "row")
    return global_top + jnp.log(summed)


def per_device_large(particles, log_weights, targets):
    row_count = particles.shape[0]
    block_count = max(1, row_count // 512)
    block_rows = row_count // block_count
    log_count = math.log(targets.shape[0] * lax.axis_size("col"))
    col_pot = jnp.zeros((targets.shape[0],), jnp.float32)
    col_lse = col_pot
    row_pot = log_weights
    for iteration in range(ITERS):
        row_pot = row_update(particles, log_weights, targets, col_pot, block_count, block_rows)
        col_lse = col_update(particles, targets, row_pot, block_count, block_rows)
        col_pot = EPS * (-log_count - col_lse)
    particles_half = particles.astype(jnp.bfloat16)
    acc = jnp.zeros(
        (lax.axis_size("row") * (targets.shape[0] // lax.axis_size("row")), particles.shape[1]),
        jnp.float32,
    )
    for index in range(block_count):
        source = particles[index * block_rows : (index + 1) * block_rows]
        potential = row_pot[index * block_rows : (index + 1) * block_rows]
        plan = jnp.exp(
            (potential[:, None] - cost_tile(source, targets)) / EPS - col_lse[None, :]
        ).astype(jnp.bfloat16)
        source_half = particles_half[index * block_rows : (index + 1) * block_rows]
        acc = acc + lax.dot_general(
            plan, source_half, (((0,), (0,)), ((), ())), preferred_element_type=jnp.float32
        )
    return lax.psum_scatter(acc, "row", scatter_dimension=0, tiled=True)


def dot_minor(a, b, precision):
    return lax.dot_general(
        a, b, (((1,), (1,)), ((), ())), precision=precision, preferred_element_type=jnp.float32
    )


def kernel(
    cols,
    x_hbm,
    w_ref,
    y_hbm,
    out_ref,
    held,
    points,
    tile,
    sums,
    part1,
    part2,
    part3,
    pots,
    local_sem,
    pair_sem,
    far_sem,
    fwd_sem,
    pot_sem,
    part_sem,
):
    rows = 4
    row = lax.axis_index("row")
    col = lax.axis_index("col")
    side = lax.rem(row, 2)
    twin = row + 1 - 2 * side
    far = lax.rem(row + 2, rows)
    far_twin = lax.rem(twin + 2, rows)
    block, feature = x_hbm.shape
    width = y_hbm.shape[0]
    total = rows * block
    groups = block // LANES
    piece = block // PIECES

    load_x = pltpu.make_async_copy(x_hbm, held.at[0], local_sem.at[0])
    load_y = pltpu.make_async_copy(y_hbm, points, local_sem.at[1])
    load_x.start()
    load_y.start()

    barrier = pltpu.get_barrier_semaphore()
    for peer in (twin, far, far_twin):
        pl.semaphore_signal(barrier, inc=1, device_id=(peer, col), device_id_type=MESH)
    for step in range(1, cols):
        pl.semaphore_signal(
            barrier, inc=1, device_id=(row, lax.rem(col + step, cols)), device_id_type=MESH
        )
    load_x.wait()
    load_y.wait()
    pl.semaphore_wait(barrier, rows - 1 + cols - 1)

    def send(src, dst, sems, index, device):
        copy = pltpu.make_async_remote_copy(
            src_ref=src,
            dst_ref=dst,
            send_sem=sems.at[0, index],
            recv_sem=sems.at[1, index],
            device_id=device,
            device_id_type=MESH,
        )
        copy.start()
        return copy

    sent = []
    far_copies = []
    for index in range(PIECES):
        span = pl.ds(index * piece, piece)
        far_copies.append(
            send(held.at[0, span], held.at[2, span], far_sem, index, (far, col))
        )
    pair_copy = send(held.at[0], held.at[1], pair_sem, 0, (twin, col))

    scale = 2.0 / (feature * EPS)
    half = 1.0 / (feature * EPS)

    def score(slot):
        source = held[slot]
        square = dot_minor(jnp.ones((8, feature), jnp.float32), source * source, HIGHEST)[:1]
        y = points[...]
        y_square = jnp.sum(y * y, axis=1, keepdims=True)
        cross = dot_minor(y * scale, source, HIGHEST)
        tile[:, slot * block : (slot + 1) * block] = cross - (y_square + square) * half

    def exchange(part, index):
        copies = []
        for step in range(1, cols):
            copies.append(
                send(
                    part.at[0],
                    part.at[step],
                    part_sem.at[index],
                    step,
                    (row, lax.rem(col + step, cols)),
                )
            )
        return copies

    score(0)
    own = tile[:, :block]
    top = jnp.max(own, axis=0, keepdims=True)
    lse = top + jnp.log(jnp.sum(jnp.exp(own - top), axis=0, keepdims=True))
    for group in range(groups):
        part1[0, group : group + 1, :] = lse[:, group * LANES : (group + 1) * LANES]
    first = exchange(part1, 0)

    pair_copy.wait_recv()
    score(1)
    forwards = []
    for index in range(PIECES):
        if index == PIECES - 1:
            for copy in first:
                copy.wait_recv()
            every = part1[:, :groups, :]
            top = jnp.max(every, axis=0)
            row_lse = top + jnp.log(jnp.sum(jnp.exp(every - top[None]), axis=0))
            weights = w_ref[...]
            pots[0, :groups, :] = weights - row_lse
            pots[0, groups : 2 * groups, :] = weights
            pot_copies = [
                send(pots.at[0], pots.at[slot], pot_sem, slot, (peer, col))
                for slot, peer in ((1, twin), (2, far), (3, far_twin))
            ]
        far_copies[index].wait_recv()
        span = pl.ds(index * piece, piece)
        forwards.append(send(held.at[2, span], held.at[3, span], fwd_sem, index, (twin, col)))
    score(2)
    for copy in forwards:
        copy.wait_recv()
    score(3)
    for copy in pot_copies:
        copy.wait_recv()

    def spread(compact):
        return jnp.concatenate([compact[g : g + 1, :] for g in range(rows * groups)], axis=1)

    def gathered(first_row):
        return jnp.concatenate(
            [pots[slot, first_row : first_row + groups, :] for slot in range(rows)], axis=0
        )

    row_pot = spread(gathered(0))
    mass = jnp.exp(gathered(groups)) * float(width * cols)

    chunks = [slice(c * CHUNK, (c + 1) * CHUNK) for c in range(width // CHUNK)]

    for rows_of in chunks:
        shifted = tile[rows_of, :] + row_pot
        tile[rows_of, :] = shifted
        fold = shifted[:, :LANES]
        for g in range(1, rows * groups):
            fold = jnp.maximum(fold, shifted[:, g * LANES : (g + 1) * LANES])
        sums[rows_of, :] = fold
    tops = jnp.max(sums[...], axis=1, keepdims=True)
    for index, rows_of in enumerate(chunks):
        entries = jnp.exp(tile[rows_of, :] - tops[rows_of])
        tile[rows_of, :] = entries
        fold = entries[:, :LANES]
        for g in range(1, rows * groups):
            fold = fold + entries[:, g * LANES : (g + 1) * LANES]
        sums[rows_of, :] = fold
    inverse = 1.0 / jnp.sum(sums[...], axis=1, keepdims=True)

    def row_sums(inverse, part):
        acc = jnp.zeros((8, total), jnp.float32)
        for rows_of in chunks:
            scaled = tile[rows_of, :] * inverse[rows_of]
            acc = acc + jnp.sum(scaled.reshape(CHUNK // 8, 8, total), axis=0)
        summed = jnp.sum(acc, axis=0, keepdims=True)
        for g in range(rows * groups):
            part[0, g : g + 1, :] = summed[:, g * LANES : (g + 1) * LANES]

    def finish(copies, part):
        for copy in copies:
            copy.wait_recv()
        return spread(mass / jnp.sum(part[...], axis=0))

    row_sums(inverse, part2)
    second = exchange(part2, 1)
    factor = finish(second, part2)

    for rows_of in chunks:
        fold = jnp.zeros((CHUNK, LANES), jnp.float32)
        for g in range(rows * groups):
            lanes = slice(g * LANES, (g + 1) * LANES)
            fold = fold + tile[rows_of, lanes] * factor[:, lanes]
        sums[rows_of, :] = fold
    inverse = 1.0 / jnp.sum(sums[...], axis=1, keepdims=True)
    row_sums(inverse, part3)
    third = exchange(part3, 2)
    source_half = held[...].reshape(total, feature).astype(jnp.bfloat16)
    factor = finish(third, part3)

    share = width // rows
    mine = tile[pl.ds(pl.multiple_of(row * share, 8), share), :] * factor
    plan = mine * (1.0 / jnp.sum(mine, axis=1, keepdims=True))
    out_ref[...] = jnp.dot(
        plan.astype(jnp.bfloat16), source_half, preferred_element_type=jnp.float32
    )

    for copy in far_copies + [pair_copy] + forwards + pot_copies + first + second + third:
        copy.wait_send()


def per_device_small(cols, particles, log_weights, targets):
    block, feature = particles.shape
    width = targets.shape[0]
    groups = block // LANES
    part = pltpu.VMEM((cols, 8, LANES), jnp.float32)
    any_space = pl.BlockSpec(memory_space=pl.ANY)
    vmem = pl.BlockSpec(memory_space=pltpu.VMEM)
    return pl.pallas_call(
        functools.partial(kernel, cols),
        out_shape=jax.ShapeDtypeStruct((width // 4, feature), jnp.float32),
        in_specs=[any_space, vmem, any_space],
        out_specs=vmem,
        scratch_shapes=[
            pltpu.VMEM((4, block, feature), jnp.float32),
            pltpu.VMEM((width, feature), jnp.float32),
            pltpu.VMEM((width, 4 * block), jnp.float32),
            pltpu.VMEM((width, LANES), jnp.float32),
            part,
            part,
            part,
            pltpu.VMEM((4, 8, LANES), jnp.float32),
            pltpu.SemaphoreType.DMA((2,)),
            pltpu.SemaphoreType.DMA((2, 1)),
            pltpu.SemaphoreType.DMA((2, PIECES)),
            pltpu.SemaphoreType.DMA((2, PIECES)),
            pltpu.SemaphoreType.DMA((2, 4)),
            pltpu.SemaphoreType.DMA((3, 2, cols)),
        ],
        compiler_params=pltpu.CompilerParams(
            collective_id=0, has_side_effects=True, vmem_limit_bytes=32 * 1024 * 1024
        ),
    )(particles, log_weights.reshape(groups, LANES), targets)


def per_device(rows, cols, particles, log_weights, targets):
    block = particles.shape[0]
    width = targets.shape[0]
    if rows == 4 and block == 2 * LANES and width % (4 * CHUNK) == 0 and width <= 2048:
        return per_device_small(cols, particles, log_weights, targets)
    return per_device_large(particles, log_weights, targets)


def solution(mesh):
    placed = (P("row", None), P("row"), P("col", None))
    return jax.shard_map(
        functools.partial(per_device, mesh.shape["row"], mesh.shape["col"]),
        mesh=mesh,
        in_specs=placed,
        out_specs=P(("col", "row"), None),
        check_vma=False,
    )
```

```python
import functools
import math

import jax
import jax.numpy as jnp
from jax import lax
from jax.experimental import pallas as pl
from jax.experimental.pallas import tpu as pltpu
from jax.sharding import PartitionSpec as P

ITERS = 3


EPS = 0.01
MESH = pl.DeviceIdType.MESH
HIGHEST = lax.Precision.HIGHEST
LANES = 128
CHUNK = 32
PIECES = 2


def cost_tile(source, points):
    source_sq = jnp.sum(source * source, axis=1)
    points_sq = jnp.sum(points * points, axis=1)
    cross = jnp.dot(source, points.T, precision=HIGHEST, preferred_element_type=jnp.float32)
    return (source_sq[:, None] + points_sq[None, :] - 2.0 * cross) / source.shape[1]


def row_update(particles, log_weights, targets, col_pot, block_count, block_rows):
    maxima = []
    totals = []
    for index in range(block_count):
        source = particles[index * block_rows : (index + 1) * block_rows]
        scores = (col_pot[None, :] - cost_tile(source, targets)) / EPS
        top = jnp.max(scores, axis=1)
        maxima.append(top)
        totals.append(jnp.sum(jnp.exp(scores - top[:, None]), axis=1))
    local_top = jnp.concatenate(maxima)
    local_sum = jnp.concatenate(totals)
    top = lax.pmax(local_top, "col")
    summed = lax.psum(local_sum * jnp.exp(local_top - top), "col")
    return EPS * (log_weights - (top + jnp.log(summed)))


def col_update(particles, targets, row_pot, block_count, block_rows):
    width = targets.shape[0]
    top = jnp.full((width,), -1e30, jnp.float32)
    summed = jnp.zeros((width,), jnp.float32)
    for index in range(block_count):
        source = particles[index * block_rows : (index + 1) * block_rows]
        potential = row_pot[index * block_rows : (index + 1) * block_rows]
        scores = (potential[:, None] - cost_tile(source, targets)) / EPS
        fresh = jnp.maximum(top, jnp.max(scores, axis=0))
        summed = summed * jnp.exp(top - fresh) + jnp.sum(jnp.exp(scores - fresh[None, :]), axis=0)
        top = fresh
    global_top = lax.pmax(top, "row")
    summed = lax.psum(summed * jnp.exp(top - global_top), "row")
    return global_top + jnp.log(summed)


def per_device_large(particles, log_weights, targets):
    row_count = particles.shape[0]
    block_count = max(1, row_count // 512)
    block_rows = row_count // block_count
    log_count = math.log(targets.shape[0] * lax.axis_size("col"))
    col_pot = jnp.zeros((targets.shape[0],), jnp.float32)
    col_lse = col_pot
    row_pot = log_weights
    for iteration in range(ITERS):
        row_pot = row_update(particles, log_weights, targets, col_pot, block_count, block_rows)
        col_lse = col_update(particles, targets, row_pot, block_count, block_rows)
        col_pot = EPS * (-log_count - col_lse)
    particles_half = particles.astype(jnp.bfloat16)
    acc = jnp.zeros(
        (lax.axis_size("row") * (targets.shape[0] // lax.axis_size("row")), particles.shape[1]),
        jnp.float32,
    )
    for index in range(block_count):
        source = particles[index * block_rows : (index + 1) * block_rows]
        potential = row_pot[index * block_rows : (index + 1) * block_rows]
        plan = jnp.exp(
            (potential[:, None] - cost_tile(source, targets)) / EPS - col_lse[None, :]
        ).astype(jnp.bfloat16)
        source_half = particles_half[index * block_rows : (index + 1) * block_rows]
        acc = acc + lax.dot_general(
            plan, source_half, (((0,), (0,)), ((), ())), preferred_element_type=jnp.float32
        )
    return lax.psum_scatter(acc, "row", scatter_dimension=0, tiled=True)


def dot_minor(a, b, precision):
    return lax.dot_general(
        a, b, (((1,), (1,)), ((), ())), precision=precision, preferred_element_type=jnp.float32
    )


def split(values):
    high = values.astype(jnp.bfloat16)
    rest = values - high.astype(jnp.float32)
    middle = rest.astype(jnp.bfloat16)
    low = (rest - middle.astype(jnp.float32)).astype(jnp.bfloat16)
    return high, middle, low


def kernel(
    cols,
    x_hbm,
    w_hbm,
    y_hbm,
    out_ref,
    held,
    points,
    weights_ref,
    point_parts,
    source_half,
    tile,
    sums,
    part1,
    part2,
    part3,
    pots,
    local_sem,
    pair_sem,
    far_sem,
    fwd_sem,
    pot_sem,
    part_sem,
):
    rows = 4
    row = lax.axis_index("row")
    col = lax.axis_index("col")
    side = lax.rem(row, 2)
    twin = row + 1 - 2 * side
    far = lax.rem(row + 2, rows)
    far_twin = lax.rem(twin + 2, rows)
    block, feature = x_hbm.shape
    width = y_hbm.shape[0]
    total = rows * block
    groups = block // LANES
    piece = block // PIECES

    load_x = pltpu.make_async_copy(x_hbm, held.at[0], local_sem.at[0])
    load_y = pltpu.make_async_copy(y_hbm, points, local_sem.at[1])
    load_w = pltpu.make_async_copy(w_hbm, weights_ref, local_sem.at[2])
    load_y.start()
    load_x.start()
    load_w.start()

    barrier = pltpu.get_barrier_semaphore()
    for peer in (twin, far, far_twin):
        pl.semaphore_signal(barrier, inc=1, device_id=(peer, col), device_id_type=MESH)
    for step in range(1, cols):
        pl.semaphore_signal(
            barrier, inc=1, device_id=(row, lax.rem(col + step, cols)), device_id_type=MESH
        )

    def send(src, dst, sems, index, device):
        copy = pltpu.make_async_remote_copy(
            src_ref=src,
            dst_ref=dst,
            send_sem=sems.at[0, index],
            recv_sem=sems.at[1, index],
            device_id=device,
            device_id_type=MESH,
        )
        copy.start()
        return copy

    scale = 2.0 / (feature * EPS)
    half = 1.0 / (feature * EPS)
    load_y.wait()
    y = points[...]
    y_square = jnp.sum(y * y, axis=1, keepdims=True) * half
    high, middle, low = split(y * scale)
    for place, part in enumerate((high, middle, high, middle, high, low)):
        point_parts[:, place * feature : (place + 1) * feature] = part

    def score(slot):
        high, middle, low = split(held[slot])
        source_half[slot * block : (slot + 1) * block, :] = high
        source_parts = jnp.concatenate([high, high, middle, middle, low, high], axis=1)
        cross = dot_minor(point_parts[...], source_parts, None)
        tile[:, slot * block : (slot + 1) * block] = cross - y_square

    def exchange(part, index):
        copies = []
        for step in range(1, cols):
            copies.append(
                send(
                    part.at[0],
                    part.at[step],
                    part_sem.at[index],
                    step,
                    (row, lax.rem(col + step, cols)),
                )
            )
        return copies

    load_x.wait()
    load_w.wait()
    score(0)
    source = held[0]
    square = dot_minor(jnp.ones((8, feature), jnp.float32), source * source, HIGHEST)[:1] * half
    own = tile[:, :block] - square
    top = jnp.max(own, axis=0, keepdims=True)
    lse = top + jnp.log(jnp.sum(jnp.exp(own - top), axis=0, keepdims=True))
    for group in range(groups):
        part1[0, group : group + 1, :] = lse[:, group * LANES : (group + 1) * LANES]

    pl.semaphore_wait(barrier, rows - 1 + cols - 1)

    first = exchange(part1, 0)
    far_copies = []
    for index in range(PIECES):
        span = pl.ds(index * piece, piece)
        far_copies.append(
            send(held.at[0, span], held.at[2, span], far_sem, index, (far, col))
        )
    pair_copy = send(held.at[0], held.at[1], pair_sem, 0, (twin, col))

    pair_copy.wait_recv()
    score(1)
    forwards = []
    for index in range(PIECES):
        if index == PIECES - 1:
            for copy in first:
                copy.wait_recv()
            every = part1[:, :groups, :]
            top = jnp.max(every, axis=0)
            row_lse = top + jnp.log(jnp.sum(jnp.exp(every - top[None]), axis=0))
            weights = weights_ref[...]
            for group in range(groups):
                pots[0, group : group + 1, :] = (weights - row_lse)[group : group + 1] - square[
                    :, group * LANES : (group + 1) * LANES
                ]
            pots[0, groups : 2 * groups, :] = weights
            pot_copies = [
                send(pots.at[0], pots.at[slot], pot_sem, slot, (peer, col))
                for slot, peer in ((1, twin), (2, far), (3, far_twin))
            ]
        far_copies[index].wait_recv()
        span = pl.ds(index * piece, piece)
        forwards.append(send(held.at[2, span], held.at[3, span], fwd_sem, index, (twin, col)))
    score(2)
    for copy in forwards:
        copy.wait_recv()
    score(3)
    for copy in pot_copies:
        copy.wait_recv()

    def spread(compact):
        return jnp.concatenate([compact[g : g + 1, :] for g in range(rows * groups)], axis=1)

    def gathered(first_row):
        return jnp.concatenate(
            [pots[slot, first_row : first_row + groups, :] for slot in range(rows)], axis=0
        )

    row_pot = spread(gathered(0))
    mass = jnp.exp(gathered(groups)) * float(width * cols)

    chunks = [slice(c * CHUNK, (c + 1) * CHUNK) for c in range(width // CHUNK)]

    for rows_of in chunks:
        shifted = tile[rows_of, :] + row_pot
        fold = shifted[:, :LANES]
        for g in range(1, rows * groups):
            fold = jnp.maximum(fold, shifted[:, g * LANES : (g + 1) * LANES])
        sums[rows_of, :] = fold
    tops = jnp.max(sums[...], axis=1, keepdims=True)
    for index, rows_of in enumerate(chunks):
        entries = jnp.exp((tile[rows_of, :] + row_pot) - tops[rows_of])
        tile[rows_of, :] = entries
        fold = entries[:, :LANES]
        for g in range(1, rows * groups):
            fold = fold + entries[:, g * LANES : (g + 1) * LANES]
        sums[rows_of, :] = fold
    inverse = 1.0 / jnp.sum(sums[...], axis=1, keepdims=True)

    def row_sums(inverse, part):
        acc = jnp.zeros((8, total), jnp.float32)
        for rows_of in chunks:
            scaled = tile[rows_of, :] * inverse[rows_of]
            acc = acc + jnp.sum(scaled.reshape(CHUNK // 8, 8, total), axis=0)
        summed = jnp.sum(acc, axis=0, keepdims=True)
        for g in range(rows * groups):
            part[0, g : g + 1, :] = summed[:, g * LANES : (g + 1) * LANES]

    def finish(copies, part):
        for copy in copies:
            copy.wait_recv()
        return spread(mass / jnp.sum(part[...], axis=0))

    row_sums(inverse, part2)
    second = exchange(part2, 1)
    factor = finish(second, part2)

    for rows_of in chunks:
        fold = jnp.zeros((CHUNK, LANES), jnp.float32)
        for g in range(rows * groups):
            lanes = slice(g * LANES, (g + 1) * LANES)
            fold = fold + tile[rows_of, lanes] * factor[:, lanes]
        sums[rows_of, :] = fold
    inverse = 1.0 / jnp.sum(sums[...], axis=1, keepdims=True)
    row_sums(inverse, part3)
    third = exchange(part3, 2)
    factor = finish(third, part3)

    share = width // rows
    mine = tile[pl.ds(pl.multiple_of(row * share, 8), share), :] * factor
    plan = mine * (1.0 / jnp.sum(mine, axis=1, keepdims=True))
    out_ref[...] = jnp.dot(
        plan.astype(jnp.bfloat16), source_half[...], preferred_element_type=jnp.float32
    )

    for copy in far_copies + [pair_copy] + forwards + pot_copies + first + second + third:
        copy.wait_send()


def per_device_small(cols, particles, log_weights, targets):
    block, feature = particles.shape
    width = targets.shape[0]
    groups = block // LANES
    part = pltpu.VMEM((cols, 8, LANES), jnp.float32)
    hbm = pl.BlockSpec(memory_space=pltpu.HBM)
    vmem = pl.BlockSpec(memory_space=pltpu.VMEM)
    return pl.pallas_call(
        functools.partial(kernel, cols),
        out_shape=jax.ShapeDtypeStruct((width // 4, feature), jnp.float32),
        in_specs=[hbm, hbm, hbm],
        out_specs=vmem,
        scratch_shapes=[
            pltpu.VMEM((4, block, feature), jnp.float32),
            pltpu.VMEM((width, feature), jnp.float32),
            pltpu.VMEM((groups, LANES), jnp.float32),
            pltpu.VMEM((width, 6 * feature), jnp.bfloat16),
            pltpu.VMEM((4 * block, feature), jnp.bfloat16),
            pltpu.VMEM((width, 4 * block), jnp.float32),
            pltpu.VMEM((width, LANES), jnp.float32),
            part,
            part,
            part,
            pltpu.VMEM((4, 8, LANES), jnp.float32),
            pltpu.SemaphoreType.DMA((3,)),
            pltpu.SemaphoreType.DMA((2, 1)),
            pltpu.SemaphoreType.DMA((2, PIECES)),
            pltpu.SemaphoreType.DMA((2, PIECES)),
            pltpu.SemaphoreType.DMA((2, 4)),
            pltpu.SemaphoreType.DMA((3, 2, cols)),
        ],
        compiler_params=pltpu.CompilerParams(
            collective_id=0, has_side_effects=True, vmem_limit_bytes=32 * 1024 * 1024
        ),
    )(particles, log_weights.reshape(groups, LANES), targets)


def per_device(rows, cols, particles, log_weights, targets):
    block = particles.shape[0]
    width = targets.shape[0]
    if rows == 4 and block == 2 * LANES and width % (4 * CHUNK) == 0 and width <= 2048:
        return per_device_small(cols, particles, log_weights, targets)
    return per_device_large(particles, log_weights, targets)


def solution(mesh):
    placed = (P("row", None), P("row"), P("col", None))
    return jax.shard_map(
        functools.partial(per_device, mesh.shape["row"], mesh.shape["col"]),
        mesh=mesh,
        in_specs=placed,
        out_specs=P(("col", "row"), None),
        check_vma=False,
    )
```

```python
import functools
import math

import jax
import jax.numpy as jnp
from jax import lax
from jax.experimental import pallas as pl
from jax.experimental.pallas import tpu as pltpu
from jax.sharding import PartitionSpec as P

ITERS = 3


EPS = 0.01
MESH = pl.DeviceIdType.MESH
HIGHEST = lax.Precision.HIGHEST
LANES = 128
CHUNK = 64
GRANT = 55168 * 1024
PIECES = 2


def cost_tile(source, points):
    source_sq = jnp.sum(source * source, axis=1)
    points_sq = jnp.sum(points * points, axis=1)
    cross = jnp.dot(source, points.T, precision=HIGHEST, preferred_element_type=jnp.float32)
    return (source_sq[:, None] + points_sq[None, :] - 2.0 * cross) / source.shape[1]


def row_update(particles, log_weights, targets, col_pot, block_count, block_rows):
    maxima = []
    totals = []
    for index in range(block_count):
        source = particles[index * block_rows : (index + 1) * block_rows]
        scores = (col_pot[None, :] - cost_tile(source, targets)) / EPS
        top = jnp.max(scores, axis=1)
        maxima.append(top)
        totals.append(jnp.sum(jnp.exp(scores - top[:, None]), axis=1))
    local_top = jnp.concatenate(maxima)
    local_sum = jnp.concatenate(totals)
    top = lax.pmax(local_top, "col")
    summed = lax.psum(local_sum * jnp.exp(local_top - top), "col")
    return EPS * (log_weights - (top + jnp.log(summed)))


def col_update(particles, targets, row_pot, block_count, block_rows):
    width = targets.shape[0]
    top = jnp.full((width,), -1e30, jnp.float32)
    summed = jnp.zeros((width,), jnp.float32)
    for index in range(block_count):
        source = particles[index * block_rows : (index + 1) * block_rows]
        potential = row_pot[index * block_rows : (index + 1) * block_rows]
        scores = (potential[:, None] - cost_tile(source, targets)) / EPS
        fresh = jnp.maximum(top, jnp.max(scores, axis=0))
        summed = summed * jnp.exp(top - fresh) + jnp.sum(jnp.exp(scores - fresh[None, :]), axis=0)
        top = fresh
    global_top = lax.pmax(top, "row")
    summed = lax.psum(summed * jnp.exp(top - global_top), "row")
    return global_top + jnp.log(summed)


def per_device_large(particles, log_weights, targets):
    row_count = particles.shape[0]
    block_count = max(1, row_count // 512)
    block_rows = row_count // block_count
    log_count = math.log(targets.shape[0] * lax.axis_size("col"))
    col_pot = jnp.zeros((targets.shape[0],), jnp.float32)
    col_lse = col_pot
    row_pot = log_weights
    for iteration in range(ITERS):
        row_pot = row_update(particles, log_weights, targets, col_pot, block_count, block_rows)
        col_lse = col_update(particles, targets, row_pot, block_count, block_rows)
        col_pot = EPS * (-log_count - col_lse)
    particles_half = particles.astype(jnp.bfloat16)
    acc = jnp.zeros(
        (lax.axis_size("row") * (targets.shape[0] // lax.axis_size("row")), particles.shape[1]),
        jnp.float32,
    )
    for index in range(block_count):
        source = particles[index * block_rows : (index + 1) * block_rows]
        potential = row_pot[index * block_rows : (index + 1) * block_rows]
        plan = jnp.exp(
            (potential[:, None] - cost_tile(source, targets)) / EPS - col_lse[None, :]
        ).astype(jnp.bfloat16)
        source_half = particles_half[index * block_rows : (index + 1) * block_rows]
        acc = acc + lax.dot_general(
            plan, source_half, (((0,), (0,)), ((), ())), preferred_element_type=jnp.float32
        )
    return lax.psum_scatter(acc, "row", scatter_dimension=0, tiled=True)


def dot_minor(a, b, precision):
    return lax.dot_general(
        a, b, (((1,), (1,)), ((), ())), precision=precision, preferred_element_type=jnp.float32
    )


def split(values):
    high = values.astype(jnp.bfloat16)
    rest = values - high.astype(jnp.float32)
    middle = rest.astype(jnp.bfloat16)
    low = (rest - middle.astype(jnp.float32)).astype(jnp.bfloat16)
    return high, middle, low


def kernel(
    cols,
    x_hbm,
    w_hbm,
    y_hbm,
    out_ref,
    held,
    points,
    weights_ref,
    point_parts,
    source_half,
    tile,
    sums,
    tops,
    part1,
    part2,
    part3,
    pots,
    local_sem,
    pair_sem,
    far_sem,
    fwd_sem,
    pot_sem,
    part_sem,
):
    rows = 4
    row = lax.axis_index("row")
    col = lax.axis_index("col")
    side = lax.rem(row, 2)
    twin = row + 1 - 2 * side
    far = lax.rem(row + 2, rows)
    far_twin = lax.rem(twin + 2, rows)
    block, feature = x_hbm.shape
    width = y_hbm.shape[0]
    total = rows * block
    groups = block // LANES
    piece = block // PIECES

    load_x = pltpu.make_async_copy(x_hbm, held.at[0], local_sem.at[0])
    load_y = pltpu.make_async_copy(y_hbm, points, local_sem.at[1])
    load_w = pltpu.make_async_copy(w_hbm, weights_ref, local_sem.at[2])
    load_y.start()
    load_x.start()
    load_w.start()

    barrier = pltpu.get_barrier_semaphore()
    for peer in (twin, far, far_twin):
        pl.semaphore_signal(barrier, inc=1, device_id=(peer, col), device_id_type=MESH)
    for step in range(1, cols):
        pl.semaphore_signal(
            barrier, inc=1, device_id=(row, lax.rem(col + step, cols)), device_id_type=MESH
        )

    def send(src, dst, sems, index, device):
        copy = pltpu.make_async_remote_copy(
            src_ref=src,
            dst_ref=dst,
            send_sem=sems.at[0, index],
            recv_sem=sems.at[1, index],
            device_id=device,
            device_id_type=MESH,
        )
        copy.start()
        return copy

    scale = 2.0 / (feature * EPS)
    half = 1.0 / (feature * EPS)
    load_y.wait()
    y = points[...]
    y_square = jnp.sum(y * y, axis=1, keepdims=True) * half
    high, middle, low = split(y * scale)
    for place, part in enumerate((high, middle, high, middle, high, low)):
        point_parts[:, place * feature : (place + 1) * feature] = part

    def score(slot, start=0, size=block):
        high, middle, low = split(held[slot, start : start + size])
        first_lane = slot * block + start
        source_half[first_lane : first_lane + size, :] = high
        source_parts = jnp.concatenate([high, high, middle, middle, low, high], axis=1)
        cross = dot_minor(point_parts[...], source_parts, None)
        tile[:, first_lane : first_lane + size] = cross - y_square

    def exchange(part, index):
        copies = []
        for step in range(1, cols):
            copies.append(
                send(
                    part.at[0],
                    part.at[step],
                    part_sem.at[index],
                    step,
                    (row, lax.rem(col + step, cols)),
                )
            )
        return copies

    load_x.wait()
    load_w.wait()
    score(0)
    source = held[0]
    square = dot_minor(jnp.ones((8, feature), jnp.float32), source * source, HIGHEST)[:1] * half
    own = tile[:, :block] - square
    top = jnp.max(own, axis=0, keepdims=True)
    lse = top + jnp.log(jnp.sum(jnp.exp(own - top), axis=0, keepdims=True))
    for group in range(groups):
        part1[0, group : group + 1, :] = lse[:, group * LANES : (group + 1) * LANES]

    pl.semaphore_wait(barrier, rows - 1 + cols - 1)

    first = exchange(part1, 0)
    far_copies = []
    for index in range(PIECES):
        span = pl.ds(index * piece, piece)
        far_copies.append(
            send(held.at[0, span], held.at[2, span], far_sem, index, (far, col))
        )
    pair_copy = send(held.at[0], held.at[1], pair_sem, 0, (twin, col))

    pair_copy.wait_recv()
    score(1)
    forwards = []
    for index in range(PIECES):
        far_copies[index].wait_recv()
        span = pl.ds(index * piece, piece)
        forwards.append(send(held.at[2, span], held.at[3, span], fwd_sem, index, (twin, col)))
        if index == 0:
            for copy in first:
                copy.wait_recv()
            every = part1[:, :groups, :]
            top = jnp.max(every, axis=0)
            row_lse = top + jnp.log(jnp.sum(jnp.exp(every - top[None]), axis=0))
            weights = weights_ref[...]
            for group in range(groups):
                pots[0, group : group + 1, :] = (weights - row_lse)[group : group + 1] - square[
                    :, group * LANES : (group + 1) * LANES
                ]
            pots[0, groups : 2 * groups, :] = weights
            pot_copies = [
                send(pots.at[0], pots.at[slot], pot_sem, slot, (peer, col))
                for slot, peer in ((1, twin), (2, far), (3, far_twin))
            ]
        score(2, index * piece, piece)
    for index in range(PIECES):
        forwards[index].wait_recv()
        score(3, index * piece, piece)
    for copy in pot_copies:
        copy.wait_recv()

    def spread(compact):
        return jnp.concatenate(
            [jnp.broadcast_to(compact[g : g + 1, :], (8, LANES)) for g in range(rows * groups)],
            axis=1,
        )

    def gathered(first_row):
        return jnp.concatenate(
            [pots[slot, first_row : first_row + groups, :] for slot in range(rows)], axis=0
        )

    def chunk_at(index):
        return pl.ds(pl.multiple_of(index * CHUNK, CHUNK), CHUNK)

    def sweep(body):
        def step(index, carry):
            body(chunk_at(index))
            return carry

        lax.fori_loop(0, width // CHUNK, step, 0)

    def by_eight(values):
        return values.reshape(CHUNK // 8, 8, values.shape[-1])

    def fold(values, combine):
        lanes = [values[..., g * LANES : (g + 1) * LANES] for g in range(rows * groups)]
        return functools.reduce(combine, lanes).reshape(CHUNK, LANES)

    row_pot = spread(gathered(0))[None]
    mass = jnp.exp(gathered(groups)) * float(width * cols)

    def largest(chunk):
        sums[chunk, :] = fold(by_eight(tile[chunk, :]) + row_pot, jnp.maximum)

    def entries(chunk):
        shifted = (by_eight(tile[chunk, :]) + row_pot) - by_eight(tops[chunk, :])
        values = jnp.exp(shifted)
        tile[chunk, :] = values.reshape(CHUNK, total)
        sums[chunk, :] = fold(values, jnp.add)

    def column_sums(factor):
        def body(chunk):
            sums[chunk, :] = fold(by_eight(tile[chunk, :]) * factor[None], jnp.add)

        sweep(body)

    def invert():
        tops[...] = 1.0 / jnp.sum(sums[...], axis=1, keepdims=True)

    def row_sums(part):
        def step(index, acc):
            chunk = chunk_at(index)
            return acc + jnp.sum(by_eight(tile[chunk, :]) * by_eight(tops[chunk, :]), axis=0)

        acc = lax.fori_loop(0, width // CHUNK, step, jnp.zeros((8, total), jnp.float32))
        summed = jnp.sum(acc, axis=0, keepdims=True)
        for g in range(rows * groups):
            part[0, g : g + 1, :] = summed[:, g * LANES : (g + 1) * LANES]

    def finish(copies, part):
        for copy in copies:
            copy.wait_recv()
        return spread(mass / jnp.sum(part[...], axis=0))

    sweep(largest)
    tops[...] = jnp.max(sums[...], axis=1, keepdims=True)
    sweep(entries)
    invert()
    row_sums(part2)
    second = exchange(part2, 1)
    column_sums(finish(second, part2))
    invert()
    row_sums(part3)
    third = exchange(part3, 2)
    factor = finish(third, part3)

    share = width // rows
    mine = tile[pl.ds(pl.multiple_of(row * share, 8), share), :]
    mine = (mine.reshape(share // 8, 8, total) * factor[None]).reshape(share, total)
    plan = mine * (1.0 / jnp.sum(mine, axis=1, keepdims=True))
    out_ref[...] = jnp.dot(
        plan.astype(jnp.bfloat16), source_half[...], preferred_element_type=jnp.float32
    )

    for copy in far_copies + [pair_copy] + forwards + pot_copies + first + second + third:
        copy.wait_send()


def per_device_small(cols, particles, log_weights, targets):
    block, feature = particles.shape
    width = targets.shape[0]
    groups = block // LANES
    part = pltpu.VMEM((cols, 8, LANES), jnp.float32)
    hbm = pl.BlockSpec(memory_space=pltpu.HBM)
    vmem = pl.BlockSpec(memory_space=pltpu.VMEM)
    return pl.pallas_call(
        functools.partial(kernel, cols),
        out_shape=jax.ShapeDtypeStruct((width // 4, feature), jnp.float32),
        in_specs=[hbm, hbm, hbm],
        out_specs=vmem,
        scratch_shapes=[
            pltpu.VMEM((4, block, feature), jnp.float32),
            pltpu.VMEM((width, feature), jnp.float32),
            pltpu.VMEM((groups, LANES), jnp.float32),
            pltpu.VMEM((width, 6 * feature), jnp.bfloat16),
            pltpu.VMEM((4 * block, feature), jnp.bfloat16),
            pltpu.VMEM((width, 4 * block), jnp.float32),
            pltpu.VMEM((width, LANES), jnp.float32),
            pltpu.VMEM((width, 1), jnp.float32),
            part,
            part,
            part,
            pltpu.VMEM((4, 8, LANES), jnp.float32),
            pltpu.SemaphoreType.DMA((3,)),
            pltpu.SemaphoreType.DMA((2, 1)),
            pltpu.SemaphoreType.DMA((2, PIECES)),
            pltpu.SemaphoreType.DMA((2, PIECES)),
            pltpu.SemaphoreType.DMA((2, 4)),
            pltpu.SemaphoreType.DMA((3, 2, cols)),
        ],
        compiler_params=pltpu.CompilerParams(
            collective_id=0, has_side_effects=True, vmem_limit_bytes=GRANT
        ),
    )(particles, log_weights.reshape(groups, LANES), targets)


def per_device(rows, cols, particles, log_weights, targets):
    block = particles.shape[0]
    width = targets.shape[0]
    if rows == 4 and block == 2 * LANES and width % CHUNK == 0 and width % 64 == 0 and width <= 1024:
        return per_device_small(cols, particles, log_weights, targets)
    return per_device_large(particles, log_weights, targets)


def solution(mesh):
    placed = (P("row", None), P("row"), P("col", None))
    return jax.shard_map(
        functools.partial(per_device, mesh.shape["row"], mesh.shape["col"]),
        mesh=mesh,
        in_specs=placed,
        out_specs=P(("col", "row"), None),
        check_vma=False,
    )
```

```python
import functools
import math

import jax
import jax.numpy as jnp
from jax import lax
from jax.experimental import pallas as pl
from jax.experimental.pallas import tpu as pltpu
from jax.sharding import PartitionSpec as P

ITERS = 3


EPS = 0.01
MESH = pl.DeviceIdType.MESH
HIGHEST = lax.Precision.HIGHEST
LANES = 128
CHUNK = 64
GRANT = 55168 * 1024
PIECES = 2


def cost_tile(source, points):
    source_sq = jnp.sum(source * source, axis=1)
    points_sq = jnp.sum(points * points, axis=1)
    cross = jnp.dot(source, points.T, precision=HIGHEST, preferred_element_type=jnp.float32)
    return (source_sq[:, None] + points_sq[None, :] - 2.0 * cross) / source.shape[1]


def row_update(particles, log_weights, targets, col_pot, block_count, block_rows):
    maxima = []
    totals = []
    for index in range(block_count):
        source = particles[index * block_rows : (index + 1) * block_rows]
        scores = (col_pot[None, :] - cost_tile(source, targets)) / EPS
        top = jnp.max(scores, axis=1)
        maxima.append(top)
        totals.append(jnp.sum(jnp.exp(scores - top[:, None]), axis=1))
    local_top = jnp.concatenate(maxima)
    local_sum = jnp.concatenate(totals)
    top = lax.pmax(local_top, "col")
    summed = lax.psum(local_sum * jnp.exp(local_top - top), "col")
    return EPS * (log_weights - (top + jnp.log(summed)))


def col_update(particles, targets, row_pot, block_count, block_rows):
    width = targets.shape[0]
    top = jnp.full((width,), -1e30, jnp.float32)
    summed = jnp.zeros((width,), jnp.float32)
    for index in range(block_count):
        source = particles[index * block_rows : (index + 1) * block_rows]
        potential = row_pot[index * block_rows : (index + 1) * block_rows]
        scores = (potential[:, None] - cost_tile(source, targets)) / EPS
        fresh = jnp.maximum(top, jnp.max(scores, axis=0))
        summed = summed * jnp.exp(top - fresh) + jnp.sum(jnp.exp(scores - fresh[None, :]), axis=0)
        top = fresh
    global_top = lax.pmax(top, "row")
    summed = lax.psum(summed * jnp.exp(top - global_top), "row")
    return global_top + jnp.log(summed)


def per_device_large(particles, log_weights, targets):
    row_count = particles.shape[0]
    block_count = max(1, row_count // 512)
    block_rows = row_count // block_count
    log_count = math.log(targets.shape[0] * lax.axis_size("col"))
    col_pot = jnp.zeros((targets.shape[0],), jnp.float32)
    col_lse = col_pot
    row_pot = log_weights
    for iteration in range(ITERS):
        row_pot = row_update(particles, log_weights, targets, col_pot, block_count, block_rows)
        col_lse = col_update(particles, targets, row_pot, block_count, block_rows)
        col_pot = EPS * (-log_count - col_lse)
    particles_half = particles.astype(jnp.bfloat16)
    acc = jnp.zeros(
        (lax.axis_size("row") * (targets.shape[0] // lax.axis_size("row")), particles.shape[1]),
        jnp.float32,
    )
    for index in range(block_count):
        source = particles[index * block_rows : (index + 1) * block_rows]
        potential = row_pot[index * block_rows : (index + 1) * block_rows]
        plan = jnp.exp(
            (potential[:, None] - cost_tile(source, targets)) / EPS - col_lse[None, :]
        ).astype(jnp.bfloat16)
        source_half = particles_half[index * block_rows : (index + 1) * block_rows]
        acc = acc + lax.dot_general(
            plan, source_half, (((0,), (0,)), ((), ())), preferred_element_type=jnp.float32
        )
    return lax.psum_scatter(acc, "row", scatter_dimension=0, tiled=True)


def dot_minor(a, b, precision):
    return lax.dot_general(
        a, b, (((1,), (1,)), ((), ())), precision=precision, preferred_element_type=jnp.float32
    )


def split(values):
    high = values.astype(jnp.bfloat16)
    rest = values - high.astype(jnp.float32)
    middle = rest.astype(jnp.bfloat16)
    low = (rest - middle.astype(jnp.float32)).astype(jnp.bfloat16)
    return high, middle, low


def kernel(
    cols,
    x_hbm,
    w_hbm,
    y_hbm,
    out_ref,
    held,
    points,
    weights_ref,
    point_parts,
    source_half,
    tile,
    sums,
    tops,
    part1,
    part2,
    part3,
    pots,
    local_sem,
    pair_sem,
    far_sem,
    fwd_sem,
    pot_sem,
    part_sem,
):
    rows = 4
    row = lax.axis_index("row")
    col = lax.axis_index("col")
    side = lax.rem(row, 2)
    twin = row + 1 - 2 * side
    far = lax.rem(row + 2, rows)
    far_twin = lax.rem(twin + 2, rows)
    block, feature = x_hbm.shape
    width = y_hbm.shape[0]
    total = rows * block
    groups = block // LANES
    piece = block // PIECES

    load_x = pltpu.make_async_copy(x_hbm, held.at[0], local_sem.at[0])
    load_y = pltpu.make_async_copy(y_hbm, points, local_sem.at[1])
    load_w = pltpu.make_async_copy(w_hbm, weights_ref, local_sem.at[2])
    load_y.start()
    load_x.start()
    load_w.start()

    barrier = pltpu.get_barrier_semaphore()
    for peer in (twin, far, far_twin):
        pl.semaphore_signal(barrier, inc=1, device_id=(peer, col), device_id_type=MESH)
    for step in range(1, cols):
        pl.semaphore_signal(
            barrier, inc=1, device_id=(row, lax.rem(col + step, cols)), device_id_type=MESH
        )

    def send(src, dst, sems, index, device):
        copy = pltpu.make_async_remote_copy(
            src_ref=src,
            dst_ref=dst,
            send_sem=sems.at[0, index],
            recv_sem=sems.at[1, index],
            device_id=device,
            device_id_type=MESH,
        )
        copy.start()
        return copy

    pl.semaphore_wait(barrier, rows - 1 + cols - 1)
    far_copies = []
    for index in range(PIECES):
        span = pl.ds(index * piece, piece)
        far_copies.append(send(x_hbm.at[span], held.at[2, span], far_sem, index, (far, col)))
    pair_copy = send(x_hbm, held.at[1], pair_sem, 0, (twin, col))

    scale = 2.0 / (feature * EPS)
    half = 1.0 / (feature * EPS)
    load_y.wait()
    y = points[...]
    y_square = jnp.sum(y * y, axis=1, keepdims=True) * half
    high, middle, low = split(y * scale)
    for place, part in enumerate((high, middle, high, middle, high, low)):
        point_parts[:, place * feature : (place + 1) * feature] = part

    def score(slot, start=0, size=block):
        high, middle, low = split(held[slot, start : start + size])
        first_lane = slot * block + start
        source_half[first_lane : first_lane + size, :] = high
        source_parts = jnp.concatenate([high, high, middle, middle, low, high], axis=1)
        cross = dot_minor(point_parts[...], source_parts, None)
        tile[:, first_lane : first_lane + size] = cross - y_square

    def exchange(part, index):
        copies = []
        for step in range(1, cols):
            copies.append(
                send(
                    part.at[0],
                    part.at[step],
                    part_sem.at[index],
                    step,
                    (row, lax.rem(col + step, cols)),
                )
            )
        return copies

    load_x.wait()
    load_w.wait()
    score(0)
    source = held[0]
    square_parts = jnp.concatenate(split(source * source), axis=1)
    square = dot_minor(jnp.ones((16, 3 * feature), jnp.bfloat16), square_parts, None)[:1] * half
    own = tile[:, :block] - square
    top = jnp.max(own, axis=0, keepdims=True)
    lse = top + jnp.log(jnp.sum(jnp.exp(own - top), axis=0, keepdims=True))
    for group in range(groups):
        part1[0, group : group + 1, :] = lse[:, group * LANES : (group + 1) * LANES]

    first = exchange(part1, 0)

    pair_copy.wait_recv()
    score(1)
    forwards = []
    for index in range(PIECES):
        far_copies[index].wait_recv()
        span = pl.ds(index * piece, piece)
        forwards.append(send(held.at[2, span], held.at[3, span], fwd_sem, index, (twin, col)))
        if index == 0:
            for copy in first:
                copy.wait_recv()
            every = part1[:, :groups, :]
            top = jnp.max(every, axis=0)
            row_lse = top + jnp.log(jnp.sum(jnp.exp(every - top[None]), axis=0))
            weights = weights_ref[...]
            for group in range(groups):
                pots[0, group : group + 1, :] = (weights - row_lse)[group : group + 1] - square[
                    :, group * LANES : (group + 1) * LANES
                ]
            pots[0, groups : 2 * groups, :] = weights
            pot_copies = [
                send(pots.at[0], pots.at[slot], pot_sem, slot, (peer, col))
                for slot, peer in ((1, twin), (2, far), (3, far_twin))
            ]
        score(2, index * piece, piece)
    for index in range(PIECES):
        forwards[index].wait_recv()
        score(3, index * piece, piece)
    for copy in pot_copies:
        copy.wait_recv()

    def spread(compact):
        return jnp.concatenate(
            [jnp.broadcast_to(compact[g : g + 1, :], (8, LANES)) for g in range(rows * groups)],
            axis=1,
        )

    def gathered(first_row):
        return jnp.concatenate(
            [pots[slot, first_row : first_row + groups, :] for slot in range(rows)], axis=0
        )

    def chunk_at(index):
        return pl.ds(pl.multiple_of(index * CHUNK, CHUNK), CHUNK)

    def sweep(body):
        def step(index, carry):
            body(chunk_at(index))
            return carry

        lax.fori_loop(0, width // CHUNK, step, 0)

    def by_eight(values):
        return values.reshape(CHUNK // 8, 8, values.shape[-1])

    def across(chunk):
        return by_eight(jnp.concatenate([tops[chunk, :]] * (rows * groups), axis=1))

    def fold(values, combine):
        lanes = [values[..., g * LANES : (g + 1) * LANES] for g in range(rows * groups)]
        return functools.reduce(combine, lanes).reshape(CHUNK, LANES)

    row_pot = spread(gathered(0))[None]
    mass = jnp.exp(gathered(groups)) * float(width * cols)

    def largest(chunk):
        sums[chunk, :] = fold(by_eight(tile[chunk, :]) + row_pot, jnp.maximum)

    def entries(chunk):
        shifted = (by_eight(tile[chunk, :]) + row_pot) - across(chunk)
        values = jnp.exp(shifted)
        tile[chunk, :] = values.reshape(CHUNK, total)
        sums[chunk, :] = fold(values, jnp.add)

    def column_sums(factor):
        def body(chunk):
            sums[chunk, :] = fold(by_eight(tile[chunk, :]) * factor[None], jnp.add)

        sweep(body)

    def invert():
        inverse = 1.0 / jnp.sum(sums[...], axis=1, keepdims=True)
        tops[...] = jnp.broadcast_to(inverse, tops.shape)

    def row_sums(part):
        def step(index, acc):
            chunk = chunk_at(index)
            return acc + jnp.sum(by_eight(tile[chunk, :]) * across(chunk), axis=0)

        acc = lax.fori_loop(0, width // CHUNK, step, jnp.zeros((8, total), jnp.float32))
        summed = jnp.sum(acc, axis=0, keepdims=True)
        for g in range(rows * groups):
            part[0, g : g + 1, :] = summed[:, g * LANES : (g + 1) * LANES]

    def finish(copies, part):
        for copy in copies:
            copy.wait_recv()
        return spread(mass / jnp.sum(part[...], axis=0))

    sweep(largest)
    tops[...] = jnp.broadcast_to(jnp.max(sums[...], axis=1, keepdims=True), tops.shape)
    sweep(entries)
    invert()
    row_sums(part2)
    second = exchange(part2, 1)
    column_sums(finish(second, part2))
    invert()
    row_sums(part3)
    third = exchange(part3, 2)
    factor = finish(third, part3)

    share = width // rows
    mine = tile[pl.ds(pl.multiple_of(row * share, 8), share), :]
    mine = (mine.reshape(share // 8, 8, total) * factor[None]).reshape(share, total)
    plan = mine * (1.0 / jnp.sum(mine, axis=1, keepdims=True))
    out_ref[...] = jnp.dot(
        plan.astype(jnp.bfloat16), source_half[...], preferred_element_type=jnp.float32
    )

    for copy in far_copies + [pair_copy] + forwards + pot_copies + first + second + third:
        copy.wait_send()


def per_device_small(cols, particles, log_weights, targets):
    block, feature = particles.shape
    width = targets.shape[0]
    groups = block // LANES
    part = pltpu.VMEM((cols, 8, LANES), jnp.float32)
    hbm = pl.BlockSpec(memory_space=pltpu.HBM)
    vmem = pl.BlockSpec(memory_space=pltpu.VMEM)
    return pl.pallas_call(
        functools.partial(kernel, cols),
        out_shape=jax.ShapeDtypeStruct((width // 4, feature), jnp.float32),
        in_specs=[hbm, hbm, hbm],
        out_specs=vmem,
        scratch_shapes=[
            pltpu.VMEM((4, block, feature), jnp.float32),
            pltpu.VMEM((width, feature), jnp.float32),
            pltpu.VMEM((groups, LANES), jnp.float32),
            pltpu.VMEM((width, 6 * feature), jnp.bfloat16),
            pltpu.VMEM((4 * block, feature), jnp.bfloat16),
            pltpu.VMEM((width, 4 * block), jnp.float32),
            pltpu.VMEM((width, LANES), jnp.float32),
            pltpu.VMEM((width, LANES), jnp.float32),
            part,
            part,
            part,
            pltpu.VMEM((4, 8, LANES), jnp.float32),
            pltpu.SemaphoreType.DMA((3,)),
            pltpu.SemaphoreType.DMA((2, 1)),
            pltpu.SemaphoreType.DMA((2, PIECES)),
            pltpu.SemaphoreType.DMA((2, PIECES)),
            pltpu.SemaphoreType.DMA((2, 4)),
            pltpu.SemaphoreType.DMA((3, 2, cols)),
        ],
        compiler_params=pltpu.CompilerParams(
            collective_id=0, has_side_effects=True, vmem_limit_bytes=GRANT
        ),
    )(particles, log_weights.reshape(groups, LANES), targets)


def per_device(rows, cols, particles, log_weights, targets):
    block = particles.shape[0]
    width = targets.shape[0]
    if rows == 4 and block == 2 * LANES and width % CHUNK == 0 and width % 64 == 0 and width <= 1024:
        return per_device_small(cols, particles, log_weights, targets)
    return per_device_large(particles, log_weights, targets)


def solution(mesh):
    placed = (P("row", None), P("row"), P("col", None))
    return jax.shard_map(
        functools.partial(per_device, mesh.shape["row"], mesh.shape["col"]),
        mesh=mesh,
        in_specs=placed,
        out_specs=P(("col", "row"), None),
        check_vma=False,
    )
```

```python
import functools
import math

import jax
import jax.numpy as jnp
from jax import lax
from jax.experimental import pallas as pl
from jax.experimental.pallas import tpu as pltpu
from jax.sharding import PartitionSpec as P

ITERS = 3


EPS = 0.01
MESH = pl.DeviceIdType.MESH
HIGHEST = lax.Precision.HIGHEST
LANES = 128
CHUNK = 64
GRANT = 55168 * 1024
PIECES = 2


def cost_tile(source, points):
    source_sq = jnp.sum(source * source, axis=1)
    points_sq = jnp.sum(points * points, axis=1)
    cross = jnp.dot(source, points.T, precision=HIGHEST, preferred_element_type=jnp.float32)
    return (source_sq[:, None] + points_sq[None, :] - 2.0 * cross) / source.shape[1]


def row_update(particles, log_weights, targets, col_pot, block_count, block_rows):
    maxima = []
    totals = []
    for index in range(block_count):
        source = particles[index * block_rows : (index + 1) * block_rows]
        scores = (col_pot[None, :] - cost_tile(source, targets)) / EPS
        top = jnp.max(scores, axis=1)
        maxima.append(top)
        totals.append(jnp.sum(jnp.exp(scores - top[:, None]), axis=1))
    local_top = jnp.concatenate(maxima)
    local_sum = jnp.concatenate(totals)
    top = lax.pmax(local_top, "col")
    summed = lax.psum(local_sum * jnp.exp(local_top - top), "col")
    return EPS * (log_weights - (top + jnp.log(summed)))


def col_update(particles, targets, row_pot, block_count, block_rows):
    width = targets.shape[0]
    top = jnp.full((width,), -1e30, jnp.float32)
    summed = jnp.zeros((width,), jnp.float32)
    for index in range(block_count):
        source = particles[index * block_rows : (index + 1) * block_rows]
        potential = row_pot[index * block_rows : (index + 1) * block_rows]
        scores = (potential[:, None] - cost_tile(source, targets)) / EPS
        fresh = jnp.maximum(top, jnp.max(scores, axis=0))
        summed = summed * jnp.exp(top - fresh) + jnp.sum(jnp.exp(scores - fresh[None, :]), axis=0)
        top = fresh
    global_top = lax.pmax(top, "row")
    summed = lax.psum(summed * jnp.exp(top - global_top), "row")
    return global_top + jnp.log(summed)


def per_device_large(particles, log_weights, targets):
    row_count = particles.shape[0]
    block_count = max(1, row_count // 512)
    block_rows = row_count // block_count
    log_count = math.log(targets.shape[0] * lax.axis_size("col"))
    col_pot = jnp.zeros((targets.shape[0],), jnp.float32)
    col_lse = col_pot
    row_pot = log_weights
    for iteration in range(ITERS):
        row_pot = row_update(particles, log_weights, targets, col_pot, block_count, block_rows)
        col_lse = col_update(particles, targets, row_pot, block_count, block_rows)
        col_pot = EPS * (-log_count - col_lse)
    particles_half = particles.astype(jnp.bfloat16)
    acc = jnp.zeros(
        (lax.axis_size("row") * (targets.shape[0] // lax.axis_size("row")), particles.shape[1]),
        jnp.float32,
    )
    for index in range(block_count):
        source = particles[index * block_rows : (index + 1) * block_rows]
        potential = row_pot[index * block_rows : (index + 1) * block_rows]
        plan = jnp.exp(
            (potential[:, None] - cost_tile(source, targets)) / EPS - col_lse[None, :]
        ).astype(jnp.bfloat16)
        source_half = particles_half[index * block_rows : (index + 1) * block_rows]
        acc = acc + lax.dot_general(
            plan, source_half, (((0,), (0,)), ((), ())), preferred_element_type=jnp.float32
        )
    return lax.psum_scatter(acc, "row", scatter_dimension=0, tiled=True)


def dot_minor(a, b, precision):
    return lax.dot_general(
        a, b, (((1,), (1,)), ((), ())), precision=precision, preferred_element_type=jnp.float32
    )


def split(values):
    high = values.astype(jnp.bfloat16)
    rest = values - high.astype(jnp.float32)
    middle = rest.astype(jnp.bfloat16)
    low = (rest - middle.astype(jnp.float32)).astype(jnp.bfloat16)
    return high, middle, low


def kernel(
    cols,
    x_hbm,
    w_hbm,
    y_hbm,
    out_ref,
    held,
    points,
    weights_ref,
    point_parts,
    source_half,
    tile,
    sums,
    tops,
    part1,
    part2,
    part3,
    pots,
    local_sem,
    pair_sem,
    far_sem,
    fwd_sem,
    pot_sem,
    part_sem,
):
    rows = 4
    row = lax.axis_index("row")
    col = lax.axis_index("col")
    side = lax.rem(row, 2)
    twin = row + 1 - 2 * side
    far = lax.rem(row + 2, rows)
    far_twin = lax.rem(twin + 2, rows)
    block, feature = x_hbm.shape
    width = y_hbm.shape[0]
    total = rows * block
    groups = block // LANES
    piece = block // PIECES

    load_x = pltpu.make_async_copy(x_hbm, held.at[0], local_sem.at[0])
    load_y = pltpu.make_async_copy(y_hbm, points, local_sem.at[1])
    load_w = pltpu.make_async_copy(w_hbm, weights_ref, local_sem.at[2])
    load_y.start()
    load_x.start()
    load_w.start()

    barrier = pltpu.get_barrier_semaphore()
    for peer in (twin, far, far_twin):
        pl.semaphore_signal(barrier, inc=1, device_id=(peer, col), device_id_type=MESH)
    for step in range(1, cols):
        pl.semaphore_signal(
            barrier, inc=1, device_id=(row, lax.rem(col + step, cols)), device_id_type=MESH
        )

    def send(src, dst, sems, index, device):
        copy = pltpu.make_async_remote_copy(
            src_ref=src,
            dst_ref=dst,
            send_sem=sems.at[0, index],
            recv_sem=sems.at[1, index],
            device_id=device,
            device_id_type=MESH,
        )
        copy.start()
        return copy

    pl.semaphore_wait(barrier, rows - 1 + cols - 1)
    far_copies = []
    for index in range(PIECES):
        span = pl.ds(index * piece, piece)
        far_copies.append(send(x_hbm.at[span], held.at[2, span], far_sem, index, (far, col)))
    pair_copy = send(x_hbm, held.at[1], pair_sem, 0, (twin, col))

    scale = 2.0 / (feature * EPS)
    half = 1.0 / (feature * EPS)
    load_y.wait()
    y = points[...]
    y_square = jnp.sum(y * y, axis=1, keepdims=True) * half
    high, middle, low = split(y * scale)
    for place, part in enumerate((high, middle, high, middle, high, low)):
        point_parts[:, place * feature : (place + 1) * feature] = part

    def score(slot, start=0, size=block):
        high, middle, low = split(held[slot, start : start + size])
        first_lane = slot * block + start
        source_half[first_lane : first_lane + size, :] = high
        source_parts = jnp.concatenate([high, high, middle, middle, low, high], axis=1)
        cross = dot_minor(point_parts[...], source_parts, None)
        tile[:, first_lane : first_lane + size] = cross - y_square

    upper = col // (cols // 2)
    place = col + upper * (cols - 1 - 2 * col)
    order = list(range(cols - 1, cols // 2 - 1, -1))
    order += [lax.rem(place + step, cols // 2) for step in range(1, cols // 2)]
    peers = [rank + upper * (cols - 1 - 2 * rank) for rank in order]

    def exchange(part, index, size):
        copies = []
        for number, peer in enumerate(peers):
            copies.append(
                pltpu.make_async_remote_copy(
                    src_ref=part.at[col, :size],
                    dst_ref=part.at[col, :size],
                    send_sem=part_sem.at[index, 0, number],
                    recv_sem=part_sem.at[index, 1, col],
                    device_id=(row, peer),
                    device_id_type=MESH,
                )
            )
            copies[-1].start()
        return copies

    def arrive(part, index, size):
        for number, peer in enumerate(reversed(peers)):
            pltpu.make_async_remote_copy(
                src_ref=part.at[peer, :size],
                dst_ref=part.at[peer, :size],
                send_sem=part_sem.at[index, 0, number],
                recv_sem=part_sem.at[index, 1, peer],
                device_id=(row, peer),
                device_id_type=MESH,
            ).wait_recv()

    load_x.wait()
    load_w.wait()
    score(0)
    source = held[0]
    square_parts = jnp.concatenate(split(source * source), axis=1)
    square = dot_minor(jnp.ones((16, 3 * feature), jnp.bfloat16), square_parts, None)[:1] * half
    own = tile[:, :block] - square
    top = jnp.max(own, axis=0, keepdims=True)
    lse = top + jnp.log(jnp.sum(jnp.exp(own - top), axis=0, keepdims=True))
    for group in range(groups):
        part1[col, group : group + 1, :] = lse[:, group * LANES : (group + 1) * LANES]

    first = exchange(part1, 0, groups)

    pair_copy.wait_recv()
    score(1)
    forwards = []
    for index in range(PIECES):
        far_copies[index].wait_recv()
        span = pl.ds(index * piece, piece)
        forwards.append(send(held.at[2, span], held.at[3, span], fwd_sem, index, (twin, col)))
        if index == 0:
            arrive(part1, 0, groups)
            every = part1[:, :groups, :]
            top = jnp.max(every, axis=0)
            row_lse = top + jnp.log(jnp.sum(jnp.exp(every - top[None]), axis=0))
            weights = weights_ref[...]
            for group in range(groups):
                pots[0, group : group + 1, :] = (weights - row_lse)[group : group + 1] - square[
                    :, group * LANES : (group + 1) * LANES
                ]
            pots[0, groups : 2 * groups, :] = weights
            pot_copies = [
                send(
                    pots.at[0, : 2 * groups],
                    pots.at[slot, : 2 * groups],
                    pot_sem,
                    slot,
                    (peer, col),
                )
                for slot, peer in ((1, twin), (2, far), (3, far_twin))
            ]
        score(2, index * piece, piece)
    for copy in pot_copies:
        copy.wait_recv()

    def spread(compact):
        return jnp.concatenate(
            [jnp.broadcast_to(compact[g : g + 1, :], (8, LANES)) for g in range(rows * groups)],
            axis=1,
        )

    def gathered(first_row):
        return jnp.concatenate(
            [pots[slot, first_row : first_row + groups, :] for slot in range(rows)], axis=0
        )

    def chunk_at(index):
        return pl.ds(pl.multiple_of(index * CHUNK, CHUNK), CHUNK)

    def sweep(body):
        def step(index, carry):
            body(chunk_at(index))
            return carry

        lax.fori_loop(0, width // CHUNK, step, 0)

    def by_eight(values):
        return values.reshape(CHUNK // 8, 8, values.shape[-1])

    def across(chunk):
        return by_eight(jnp.concatenate([tops[chunk, :]] * (rows * groups), axis=1))

    def fold(values, combine):
        lanes = [values[..., g * LANES : (g + 1) * LANES] for g in range(values.shape[-1] // LANES)]
        return functools.reduce(combine, lanes).reshape(CHUNK, LANES)

    row_pot = spread(gathered(0))[None]
    mass = jnp.exp(gathered(groups)) * float(width * cols)

    known = (rows - 1) * block

    def largest(chunk):
        sums[chunk, :] = fold(by_eight(tile[chunk, :known]) + row_pot[..., :known], jnp.maximum)

    def largest_rest(chunk):
        rest = fold(by_eight(tile[chunk, known:]) + row_pot[..., known:], jnp.maximum)
        sums[chunk, :] = jnp.maximum(sums[chunk, :], rest)

    def entries(chunk):
        shifted = (by_eight(tile[chunk, :]) + row_pot) - across(chunk)
        values = jnp.exp(shifted)
        tile[chunk, :] = values.reshape(CHUNK, total)
        sums[chunk, :] = fold(values, jnp.add)

    def column_sums(factor):
        def body(chunk):
            sums[chunk, :] = fold(by_eight(tile[chunk, :]) * factor[None], jnp.add)

        sweep(body)

    def invert():
        inverse = 1.0 / jnp.sum(sums[...], axis=1, keepdims=True)
        tops[...] = jnp.broadcast_to(inverse, tops.shape)

    def row_sums(part):
        def step(index, acc):
            chunk = chunk_at(index)
            return acc + jnp.sum(by_eight(tile[chunk, :]) * across(chunk), axis=0)

        acc = lax.fori_loop(0, width // CHUNK, step, jnp.zeros((8, total), jnp.float32))
        summed = jnp.sum(acc, axis=0, keepdims=True)
        for g in range(rows * groups):
            part[col, g : g + 1, :] = summed[:, g * LANES : (g + 1) * LANES]

    def finish(part, index):
        arrive(part, index, rows * groups)
        return spread(mass / jnp.sum(part[...], axis=0))

    sweep(largest)
    for index in range(PIECES):
        forwards[index].wait_recv()
        score(3, index * piece, piece)
    sweep(largest_rest)
    tops[...] = jnp.broadcast_to(jnp.max(sums[...], axis=1, keepdims=True), tops.shape)
    sweep(entries)
    invert()
    row_sums(part2)
    second = exchange(part2, 1, rows * groups)
    column_sums(finish(part2, 1))
    invert()
    row_sums(part3)
    third = exchange(part3, 2, rows * groups)
    factor = finish(part3, 2)

    share = width // rows
    mine = tile[pl.ds(pl.multiple_of(row * share, 8), share), :]
    mine = (mine.reshape(share // 8, 8, total) * factor[None]).reshape(share, total)
    plan = mine * (1.0 / jnp.sum(mine, axis=1, keepdims=True))
    out_ref[...] = jnp.dot(
        plan.astype(jnp.bfloat16), source_half[...], preferred_element_type=jnp.float32
    )

    for copy in far_copies + [pair_copy] + forwards + pot_copies + first + second + third:
        copy.wait_send()


def per_device_small(cols, particles, log_weights, targets):
    block, feature = particles.shape
    width = targets.shape[0]
    groups = block // LANES
    part = pltpu.VMEM((cols, 8, LANES), jnp.float32)
    hbm = pl.BlockSpec(memory_space=pltpu.HBM)
    vmem = pl.BlockSpec(memory_space=pltpu.VMEM)
    return pl.pallas_call(
        functools.partial(kernel, cols),
        out_shape=jax.ShapeDtypeStruct((width // 4, feature), jnp.float32),
        in_specs=[hbm, hbm, hbm],
        out_specs=vmem,
        scratch_shapes=[
            pltpu.VMEM((4, block, feature), jnp.float32),
            pltpu.VMEM((width, feature), jnp.float32),
            pltpu.VMEM((groups, LANES), jnp.float32),
            pltpu.VMEM((width, 6 * feature), jnp.bfloat16),
            pltpu.VMEM((4 * block, feature), jnp.bfloat16),
            pltpu.VMEM((width, 4 * block), jnp.float32),
            pltpu.VMEM((width, LANES), jnp.float32),
            pltpu.VMEM((width, LANES), jnp.float32),
            part,
            part,
            part,
            pltpu.VMEM((4, 8, LANES), jnp.float32),
            pltpu.SemaphoreType.DMA((3,)),
            pltpu.SemaphoreType.DMA((2, 1)),
            pltpu.SemaphoreType.DMA((2, PIECES)),
            pltpu.SemaphoreType.DMA((2, PIECES)),
            pltpu.SemaphoreType.DMA((2, 4)),
            pltpu.SemaphoreType.DMA((3, 2, cols)),
        ],
        compiler_params=pltpu.CompilerParams(
            collective_id=0, has_side_effects=True, vmem_limit_bytes=GRANT
        ),
    )(particles, log_weights.reshape(groups, LANES), targets)


def per_device(rows, cols, particles, log_weights, targets):
    block = particles.shape[0]
    width = targets.shape[0]
    if rows == 4 and block == 2 * LANES and width % CHUNK == 0 and width % 64 == 0 and width <= 1024:
        return per_device_small(cols, particles, log_weights, targets)
    return per_device_large(particles, log_weights, targets)


def solution(mesh):
    placed = (P("row", None), P("row"), P("col", None))
    return jax.shard_map(
        functools.partial(per_device, mesh.shape["row"], mesh.shape["col"]),
        mesh=mesh,
        in_specs=placed,
        out_specs=P(("col", "row"), None),
        check_vma=False,
    )
```

```python
import functools
import math

import jax
import jax.numpy as jnp
from jax import lax
from jax.experimental import pallas as pl
from jax.experimental.pallas import tpu as pltpu
from jax.sharding import PartitionSpec as P

ITERS = 3


EPS = 0.01
MESH = pl.DeviceIdType.MESH
HIGHEST = lax.Precision.HIGHEST
LANES = 128
CHUNK = 64
GRANT = 55168 * 1024
PIECES = 2


def cost_tile(source, points):
    source_sq = jnp.sum(source * source, axis=1)
    points_sq = jnp.sum(points * points, axis=1)
    cross = jnp.dot(source, points.T, precision=HIGHEST, preferred_element_type=jnp.float32)
    return (source_sq[:, None] + points_sq[None, :] - 2.0 * cross) / source.shape[1]


def row_update(particles, log_weights, targets, col_pot, block_count, block_rows):
    maxima = []
    totals = []
    for index in range(block_count):
        source = particles[index * block_rows : (index + 1) * block_rows]
        scores = (col_pot[None, :] - cost_tile(source, targets)) / EPS
        top = jnp.max(scores, axis=1)
        maxima.append(top)
        totals.append(jnp.sum(jnp.exp(scores - top[:, None]), axis=1))
    local_top = jnp.concatenate(maxima)
    local_sum = jnp.concatenate(totals)
    top = lax.pmax(local_top, "col")
    summed = lax.psum(local_sum * jnp.exp(local_top - top), "col")
    return EPS * (log_weights - (top + jnp.log(summed)))


def col_update(particles, targets, row_pot, block_count, block_rows):
    width = targets.shape[0]
    top = jnp.full((width,), -1e30, jnp.float32)
    summed = jnp.zeros((width,), jnp.float32)
    for index in range(block_count):
        source = particles[index * block_rows : (index + 1) * block_rows]
        potential = row_pot[index * block_rows : (index + 1) * block_rows]
        scores = (potential[:, None] - cost_tile(source, targets)) / EPS
        fresh = jnp.maximum(top, jnp.max(scores, axis=0))
        summed = summed * jnp.exp(top - fresh) + jnp.sum(jnp.exp(scores - fresh[None, :]), axis=0)
        top = fresh
    global_top = lax.pmax(top, "row")
    summed = lax.psum(summed * jnp.exp(top - global_top), "row")
    return global_top + jnp.log(summed)


def per_device_large(particles, log_weights, targets):
    row_count = particles.shape[0]
    block_count = max(1, row_count // 512)
    block_rows = row_count // block_count
    log_count = math.log(targets.shape[0] * lax.axis_size("col"))
    col_pot = jnp.zeros((targets.shape[0],), jnp.float32)
    col_lse = col_pot
    row_pot = log_weights
    for iteration in range(ITERS):
        row_pot = row_update(particles, log_weights, targets, col_pot, block_count, block_rows)
        col_lse = col_update(particles, targets, row_pot, block_count, block_rows)
        col_pot = EPS * (-log_count - col_lse)
    particles_half = particles.astype(jnp.bfloat16)
    acc = jnp.zeros(
        (lax.axis_size("row") * (targets.shape[0] // lax.axis_size("row")), particles.shape[1]),
        jnp.float32,
    )
    for index in range(block_count):
        source = particles[index * block_rows : (index + 1) * block_rows]
        potential = row_pot[index * block_rows : (index + 1) * block_rows]
        plan = jnp.exp(
            (potential[:, None] - cost_tile(source, targets)) / EPS - col_lse[None, :]
        ).astype(jnp.bfloat16)
        source_half = particles_half[index * block_rows : (index + 1) * block_rows]
        acc = acc + lax.dot_general(
            plan, source_half, (((0,), (0,)), ((), ())), preferred_element_type=jnp.float32
        )
    return lax.psum_scatter(acc, "row", scatter_dimension=0, tiled=True)


def dot_minor(a, b, precision):
    return lax.dot_general(
        a, b, (((1,), (1,)), ((), ())), precision=precision, preferred_element_type=jnp.float32
    )


def split(values):
    high = values.astype(jnp.bfloat16)
    rest = values - high.astype(jnp.float32)
    middle = rest.astype(jnp.bfloat16)
    low = (rest - middle.astype(jnp.float32)).astype(jnp.bfloat16)
    return high, middle, low


def kernel(
    cols,
    x_hbm,
    w_hbm,
    y_hbm,
    out_ref,
    held,
    points,
    weights_ref,
    point_parts,
    source_half,
    tile,
    sums,
    tops,
    squares,
    part1,
    part2,
    part3,
    pots,
    local_sem,
    pair_sem,
    far_sem,
    fwd_sem,
    pot_sem,
    part_sem,
):
    rows = 4
    row = lax.axis_index("row")
    col = lax.axis_index("col")
    side = lax.rem(row, 2)
    twin = row + 1 - 2 * side
    far = lax.rem(row + 2, rows)
    far_twin = lax.rem(twin + 2, rows)
    block, feature = x_hbm.shape
    width = y_hbm.shape[0]
    total = rows * block
    groups = block // LANES
    piece = block // PIECES

    load_x = pltpu.make_async_copy(x_hbm, held.at[0], local_sem.at[0])
    load_y = pltpu.make_async_copy(y_hbm, points, local_sem.at[1])
    load_w = pltpu.make_async_copy(w_hbm, weights_ref, local_sem.at[2])
    load_y.start()
    load_x.start()
    load_w.start()

    def each(count, body):
        def step(index, carry):
            body(index)
            return carry

        lax.fori_loop(0, count, step, 0)

    barrier = pltpu.get_barrier_semaphore()

    def greet(peer_row, peer_col):
        pl.semaphore_signal(
            barrier, inc=1, device_id=(peer_row, peer_col), device_id_type=MESH
        )

    for peer in (twin, far, far_twin):
        greet(peer, col)
    each(cols - 1, lambda index: greet(row, lax.rem(col + index + 1, cols)))

    def link(src, dst, sems, index, device):
        return pltpu.make_async_remote_copy(
            src_ref=src,
            dst_ref=dst,
            send_sem=sems.at[0, index],
            recv_sem=sems.at[1, index],
            device_id=device,
            device_id_type=MESH,
        )

    def far_link(index):
        span = pl.ds(index * piece, piece)
        return link(x_hbm.at[span], held.at[2, span], far_sem, index, (far, col))

    def forward_link(index):
        span = pl.ds(index * piece, piece)
        return link(held.at[2, span], held.at[3, span], fwd_sem, index, (twin, col))

    pair_link = link(x_hbm, held.at[1], pair_sem, 0, (twin, col))
    pot_links = [
        link(pots.at[0], pots.at[slot], pot_sem, slot, (peer, col))
        for slot, peer in ((1, twin), (2, far), (3, far_twin))
    ]

    def part_link(part, number, index):
        return link(
            part.at[0],
            part.at[index + 1],
            part_sem.at[number],
            index + 1,
            (row, lax.rem(col + index + 1, cols)),
        )

    def exchange(part, number):
        each(cols - 1, lambda index: part_link(part, number, index).start())

    def arrive(part, number):
        each(cols - 1, lambda index: part_link(part, number, index).wait_recv())

    pl.semaphore_wait(barrier, rows - 1 + cols - 1)
    for index in range(PIECES):
        far_link(index).start()
    pair_link.start()

    scale = 2.0 / (feature * EPS)
    half = 1.0 / (feature * EPS)
    load_y.wait()

    def split_points(index):
        chunk = pl.ds(pl.multiple_of(index * CHUNK, CHUNK), CHUNK)
        y = points[chunk, :]
        square = jnp.sum(y * y, axis=1, keepdims=True) * half
        tops[chunk, :] = jnp.broadcast_to(square, (CHUNK, LANES))
        high, middle, low = split(y * scale)
        point_parts[chunk, :] = jnp.concatenate([high, middle, high, middle, high, low], axis=1)

    each(width // CHUNK, split_points)
    load_x.wait()
    load_w.wait()

    def score(slot):
        high, middle, low = split(held[slot])
        here = pl.ds(pl.multiple_of(slot * block, block), block)
        source_half[here, :] = high
        source_parts = jnp.concatenate([high, high, middle, middle, low, high], axis=1)
        cross = dot_minor(point_parts[...], source_parts, None)
        tile[:, here] = cross - jnp.concatenate([tops[...]] * groups, axis=1)

    def first_sums():
        source = held[0]
        square_parts = jnp.concatenate(split(source * source), axis=1)
        square = dot_minor(jnp.ones((16, 3 * feature), jnp.bfloat16), square_parts, None)[:1] * half
        own = tile[:, :block] - square
        top = jnp.max(own, axis=0, keepdims=True)
        lse = top + jnp.log(jnp.sum(jnp.exp(own - top), axis=0, keepdims=True))
        for group in range(groups):
            lanes = slice(group * LANES, (group + 1) * LANES)
            part1[0, group : group + 1, :] = lse[:, lanes]
            squares[group : group + 1, :] = square[:, lanes]
        exchange(part1, 0)

    def first_potential():
        arrive(part1, 0)
        every = part1[:, :groups, :]
        top = jnp.max(every, axis=0)
        row_lse = top + jnp.log(jnp.sum(jnp.exp(every - top[None]), axis=0))
        weights = weights_ref[...]
        pots[0, :groups, :] = weights - row_lse - squares[...]
        pots[0, groups : 2 * groups, :] = weights
        for copy in pot_links:
            copy.start()

    def take_block(slot):
        @pl.when(slot == 1)
        def _():
            pair_link.wait_recv()

        @pl.when(slot == 2)
        def _():
            for index in range(PIECES):
                far_link(index).wait_recv()
                forward_link(index).start()
                if index == 0:
                    first_potential()

        @pl.when(slot == 3)
        def _():
            for index in range(PIECES):
                forward_link(index).wait_recv()

        score(slot)

        @pl.when(slot == 0)
        def _():
            first_sums()

    each(rows, take_block)
    for copy in pot_links:
        copy.wait_recv()

    def spread(compact):
        return jnp.concatenate(
            [jnp.broadcast_to(compact[g : g + 1, :], (8, LANES)) for g in range(rows * groups)],
            axis=1,
        )

    def gathered(first_row):
        return jnp.concatenate(
            [pots[slot, first_row : first_row + groups, :] for slot in range(rows)], axis=0
        )

    def chunk_at(index):
        return pl.ds(pl.multiple_of(index * CHUNK, CHUNK), CHUNK)

    def sweep(body):
        each(width // CHUNK, lambda index: body(chunk_at(index)))

    def by_eight(values):
        return values.reshape(CHUNK // 8, 8, values.shape[-1])

    def across(chunk):
        return by_eight(jnp.concatenate([tops[chunk, :]] * (rows * groups), axis=1))

    def fold(values, combine):
        lanes = [values[..., g * LANES : (g + 1) * LANES] for g in range(rows * groups)]
        return functools.reduce(combine, lanes).reshape(CHUNK, LANES)

    row_pot = spread(gathered(0))[None]
    mass = jnp.exp(gathered(groups)) * float(width * cols)

    def largest(chunk):
        sums[chunk, :] = fold(by_eight(tile[chunk, :]) + row_pot, jnp.maximum)

    def entries(chunk):
        shifted = (by_eight(tile[chunk, :]) + row_pot) - across(chunk)
        values = jnp.exp(shifted)
        tile[chunk, :] = values.reshape(CHUNK, total)
        sums[chunk, :] = fold(values, jnp.add)

    def invert():
        inverse = 1.0 / jnp.sum(sums[...], axis=1, keepdims=True)
        tops[...] = jnp.broadcast_to(inverse, tops.shape)

    def row_sums(part, number):
        def step(index, acc):
            chunk = chunk_at(index)
            return acc + jnp.sum(by_eight(tile[chunk, :]) * across(chunk), axis=0)

        acc = lax.fori_loop(0, width // CHUNK, step, jnp.zeros((8, total), jnp.float32))
        summed = jnp.sum(acc, axis=0, keepdims=True)
        for g in range(rows * groups):
            part[0, g : g + 1, :] = summed[:, g * LANES : (g + 1) * LANES]
        exchange(part, number)

    def finish(part, number):
        arrive(part, number)
        return spread(mass / jnp.sum(part[...], axis=0))[None]

    sweep(largest)
    tops[...] = jnp.broadcast_to(jnp.max(sums[...], axis=1, keepdims=True), tops.shape)
    sweep(entries)
    invert()
    row_sums(part2, 1)
    factor = finish(part2, 1)

    def column_sums(chunk):
        sums[chunk, :] = fold(by_eight(tile[chunk, :]) * factor, jnp.add)

    sweep(column_sums)
    invert()
    row_sums(part3, 2)
    last_factor = finish(part3, 2)

    share = width // rows
    mine = tile[pl.ds(pl.multiple_of(row * share, 8), share), :]
    mine = (mine.reshape(share // 8, 8, total) * last_factor).reshape(share, total)
    plan = mine * (1.0 / jnp.sum(mine, axis=1, keepdims=True))
    out_ref[...] = jnp.dot(
        plan.astype(jnp.bfloat16), source_half[...], preferred_element_type=jnp.float32
    )

    for index in range(PIECES):
        far_link(index).wait_send()
        forward_link(index).wait_send()
    pair_link.wait_send()
    for copy in pot_links:
        copy.wait_send()
    for number, part in enumerate((part1, part2, part3)):
        each(cols - 1, lambda index: part_link(part, number, index).wait_send())


def per_device_small(cols, particles, log_weights, targets):
    block, feature = particles.shape
    width = targets.shape[0]
    groups = block // LANES
    part = pltpu.VMEM((cols, 8, LANES), jnp.float32)
    hbm = pl.BlockSpec(memory_space=pltpu.HBM)
    vmem = pl.BlockSpec(memory_space=pltpu.VMEM)
    return pl.pallas_call(
        functools.partial(kernel, cols),
        out_shape=jax.ShapeDtypeStruct((width // 4, feature), jnp.float32),
        in_specs=[hbm, hbm, hbm],
        out_specs=vmem,
        scratch_shapes=[
            pltpu.VMEM((4, block, feature), jnp.float32),
            pltpu.VMEM((width, feature), jnp.float32),
            pltpu.VMEM((groups, LANES), jnp.float32),
            pltpu.VMEM((width, 6 * feature), jnp.bfloat16),
            pltpu.VMEM((4 * block, feature), jnp.bfloat16),
            pltpu.VMEM((width, 4 * block), jnp.float32),
            pltpu.VMEM((width, LANES), jnp.float32),
            pltpu.VMEM((width, LANES), jnp.float32),
            pltpu.VMEM((groups, LANES), jnp.float32),
            part,
            part,
            part,
            pltpu.VMEM((4, 8, LANES), jnp.float32),
            pltpu.SemaphoreType.DMA((3,)),
            pltpu.SemaphoreType.DMA((2, 1)),
            pltpu.SemaphoreType.DMA((2, PIECES)),
            pltpu.SemaphoreType.DMA((2, PIECES)),
            pltpu.SemaphoreType.DMA((2, 4)),
            pltpu.SemaphoreType.DMA((3, 2, cols)),
        ],
        compiler_params=pltpu.CompilerParams(
            collective_id=0, has_side_effects=True, vmem_limit_bytes=GRANT
        ),
    )(particles, log_weights.reshape(groups, LANES), targets)


def per_device(rows, cols, particles, log_weights, targets):
    block = particles.shape[0]
    width = targets.shape[0]
    if rows == 4 and block == 2 * LANES and width % CHUNK == 0 and width % 64 == 0 and width <= 1024:
        return per_device_small(cols, particles, log_weights, targets)
    return per_device_large(particles, log_weights, targets)


def solution(mesh):
    placed = (P("row", None), P("row"), P("col", None))
    return jax.shard_map(
        functools.partial(per_device, mesh.shape["row"], mesh.shape["col"]),
        mesh=mesh,
        in_specs=placed,
        out_specs=P(("col", "row"), None),
        check_vma=False,
    )
```

```python
import functools
import math

import jax
import jax.numpy as jnp
from jax import lax
from jax.experimental import pallas as pl
from jax.experimental.pallas import tpu as pltpu
from jax.sharding import PartitionSpec as P

ITERS = 3


EPS = 0.01
MESH = pl.DeviceIdType.MESH
HIGHEST = lax.Precision.HIGHEST
LANES = 128
CHUNK = 64
GRANT = 55168 * 1024
PIECES = 2


def cost_tile(source, points):
    source_sq = jnp.sum(source * source, axis=1)
    points_sq = jnp.sum(points * points, axis=1)
    cross = jnp.dot(source, points.T, precision=HIGHEST, preferred_element_type=jnp.float32)
    return (source_sq[:, None] + points_sq[None, :] - 2.0 * cross) / source.shape[1]


def row_update(particles, log_weights, targets, col_pot, block_count, block_rows):
    maxima = []
    totals = []
    for index in range(block_count):
        source = particles[index * block_rows : (index + 1) * block_rows]
        scores = (col_pot[None, :] - cost_tile(source, targets)) / EPS
        top = jnp.max(scores, axis=1)
        maxima.append(top)
        totals.append(jnp.sum(jnp.exp(scores - top[:, None]), axis=1))
    local_top = jnp.concatenate(maxima)
    local_sum = jnp.concatenate(totals)
    top = lax.pmax(local_top, "col")
    summed = lax.psum(local_sum * jnp.exp(local_top - top), "col")
    return EPS * (log_weights - (top + jnp.log(summed)))


def col_update(particles, targets, row_pot, block_count, block_rows):
    width = targets.shape[0]
    top = jnp.full((width,), -1e30, jnp.float32)
    summed = jnp.zeros((width,), jnp.float32)
    for index in range(block_count):
        source = particles[index * block_rows : (index + 1) * block_rows]
        potential = row_pot[index * block_rows : (index + 1) * block_rows]
        scores = (potential[:, None] - cost_tile(source, targets)) / EPS
        fresh = jnp.maximum(top, jnp.max(scores, axis=0))
        summed = summed * jnp.exp(top - fresh) + jnp.sum(jnp.exp(scores - fresh[None, :]), axis=0)
        top = fresh
    global_top = lax.pmax(top, "row")
    summed = lax.psum(summed * jnp.exp(top - global_top), "row")
    return global_top + jnp.log(summed)


def per_device_large(particles, log_weights, targets):
    row_count = particles.shape[0]
    block_count = max(1, row_count // 512)
    block_rows = row_count // block_count
    log_count = math.log(targets.shape[0] * lax.axis_size("col"))
    col_pot = jnp.zeros((targets.shape[0],), jnp.float32)
    col_lse = col_pot
    row_pot = log_weights
    for iteration in range(ITERS):
        row_pot = row_update(particles, log_weights, targets, col_pot, block_count, block_rows)
        col_lse = col_update(particles, targets, row_pot, block_count, block_rows)
        col_pot = EPS * (-log_count - col_lse)
    particles_half = particles.astype(jnp.bfloat16)
    acc = jnp.zeros(
        (lax.axis_size("row") * (targets.shape[0] // lax.axis_size("row")), particles.shape[1]),
        jnp.float32,
    )
    for index in range(block_count):
        source = particles[index * block_rows : (index + 1) * block_rows]
        potential = row_pot[index * block_rows : (index + 1) * block_rows]
        plan = jnp.exp(
            (potential[:, None] - cost_tile(source, targets)) / EPS - col_lse[None, :]
        ).astype(jnp.bfloat16)
        source_half = particles_half[index * block_rows : (index + 1) * block_rows]
        acc = acc + lax.dot_general(
            plan, source_half, (((0,), (0,)), ((), ())), preferred_element_type=jnp.float32
        )
    return lax.psum_scatter(acc, "row", scatter_dimension=0, tiled=True)


def dot_minor(a, b, precision):
    return lax.dot_general(
        a, b, (((1,), (1,)), ((), ())), precision=precision, preferred_element_type=jnp.float32
    )


def split(values):
    high = values.astype(jnp.bfloat16)
    rest = values - high.astype(jnp.float32)
    middle = rest.astype(jnp.bfloat16)
    low = (rest - middle.astype(jnp.float32)).astype(jnp.bfloat16)
    return high, middle, low


def kernel(
    cols,
    x_hbm,
    w_hbm,
    y_hbm,
    out_ref,
    held,
    points,
    weights_ref,
    point_parts,
    source_half,
    tile,
    sums,
    tops,
    part1,
    part2,
    part3,
    pots,
    local_sem,
    pair_sem,
    far_sem,
    fwd_sem,
    pot_sem,
    part_sem,
    first_sem,
):
    rows = 4
    row = lax.axis_index("row")
    col = lax.axis_index("col")
    side = lax.rem(row, 2)
    twin = row + 1 - 2 * side
    far = lax.rem(row + 2, rows)
    far_twin = lax.rem(twin + 2, rows)
    block, feature = x_hbm.shape
    width = y_hbm.shape[0]
    total = rows * block
    groups = block // LANES
    piece = block // PIECES

    load_x = pltpu.make_async_copy(x_hbm, held.at[0], local_sem.at[0])
    load_y = pltpu.make_async_copy(y_hbm, points, local_sem.at[1])
    load_w = pltpu.make_async_copy(w_hbm, weights_ref, local_sem.at[2])
    load_y.start()
    load_x.start()
    load_w.start()

    barrier = pltpu.get_barrier_semaphore()
    family = (row, twin, far, far_twin)

    def greet(peer_row, peer_col):
        pl.semaphore_signal(
            barrier, inc=1, device_id=(peer_row, peer_col), device_id_type=MESH
        )

    def greet_step(step, carry):
        for peer in family:
            greet(peer, lax.rem(col + step, cols))
        return carry

    for peer in family[1:]:
        greet(peer, col)
    lax.fori_loop(1, cols, greet_step, 0)

    def send(src, dst, sems, index, device):
        copy = pltpu.make_async_remote_copy(
            src_ref=src,
            dst_ref=dst,
            send_sem=sems.at[0, index],
            recv_sem=sems.at[1, index],
            device_id=device,
            device_id_type=MESH,
        )
        copy.start()
        return copy

    pl.semaphore_wait(barrier, rows * cols - 1)
    far_copies = []
    for index in range(PIECES):
        span = pl.ds(index * piece, piece)
        far_copies.append(send(x_hbm.at[span], held.at[2, span], far_sem, index, (far, col)))
    pair_copy = send(x_hbm, held.at[1], pair_sem, 0, (twin, col))

    scale = 2.0 / (feature * EPS)
    half = 1.0 / (feature * EPS)
    load_y.wait()
    y = points[...]
    y_square = jnp.sum(y * y, axis=1, keepdims=True) * half
    high, middle, low = split(y * scale)
    for place, part in enumerate((high, middle, high, middle, high, low)):
        point_parts[:, place * feature : (place + 1) * feature] = part

    def score(slot, start=0, size=block):
        high, middle, low = split(held[slot, start : start + size])
        first_lane = slot * block + start
        source_half[first_lane : first_lane + size, :] = high
        source_parts = jnp.concatenate([high, high, middle, middle, low, high], axis=1)
        cross = dot_minor(point_parts[...], source_parts, None)
        tile[:, first_lane : first_lane + size] = cross - y_square

    def exchange(part, index):
        copies = []
        for step in range(1, cols):
            copies.append(
                send(
                    part.at[0],
                    part.at[step],
                    part_sem.at[index],
                    step,
                    (row, lax.rem(col + step, cols)),
                )
            )
        return copies

    load_x.wait()
    load_w.wait()
    source = held[0]
    square_parts = jnp.concatenate(split(source * source), axis=1)
    square = dot_minor(jnp.ones((16, 3 * feature), jnp.bfloat16), square_parts, None)[:1] * half
    for group in range(groups):
        pots[0, group : group + 1, :] = square[:, group * LANES : (group + 1) * LANES]
    pots[0, groups : 2 * groups, :] = weights_ref[...]
    pot_copies = [
        send(pots.at[0, : 2 * groups], pots.at[slot, : 2 * groups], pot_sem, slot, (peer, col))
        for slot, peer in ((1, twin), (2, far), (3, far_twin))
    ]
    score(0)
    own = tile[:, :block] - square
    top = jnp.max(own, axis=0, keepdims=True)
    lse = top + jnp.log(jnp.sum(jnp.exp(own - top), axis=0, keepdims=True))
    for group in range(groups):
        part1[0, group : group + 1, :] = lse[:, group * LANES : (group + 1) * LANES]

    def first_link(slot, step):
        return pltpu.make_async_remote_copy(
            src_ref=part1.at[0, :groups],
            dst_ref=part1.at[step, slot * groups : (slot + 1) * groups],
            send_sem=first_sem.at[0, slot, step],
            recv_sem=first_sem.at[1, slot, step],
            device_id=(family[slot], lax.rem(col + step, cols)),
            device_id_type=MESH,
        )

    def each_first(action):
        def body(step, carry):
            for slot in range(rows):
                action(first_link(slot, step))
            return carry

        lax.fori_loop(1, cols, body, 0)
        for slot in range(1, rows):
            action(first_link(slot, 0))

    each_first(lambda copy: copy.start())

    pair_copy.wait_recv()
    score(1)
    forwards = []
    for index in range(PIECES):
        far_copies[index].wait_recv()
        span = pl.ds(index * piece, piece)
        forwards.append(send(held.at[2, span], held.at[3, span], fwd_sem, index, (twin, col)))
        score(2, index * piece, piece)
    for index in range(PIECES):
        forwards[index].wait_recv()
        score(3, index * piece, piece)
    for copy in pot_copies:
        copy.wait_recv()
    each_first(lambda copy: copy.wait_recv())

    def spread(compact):
        return jnp.concatenate(
            [jnp.broadcast_to(compact[g : g + 1, :], (8, LANES)) for g in range(rows * groups)],
            axis=1,
        )

    def gathered(first_row):
        return jnp.concatenate(
            [pots[slot, first_row : first_row + groups, :] for slot in range(rows)], axis=0
        )

    def chunk_at(index):
        return pl.ds(pl.multiple_of(index * CHUNK, CHUNK), CHUNK)

    def sweep(body):
        def step(index, carry):
            body(chunk_at(index))
            return carry

        lax.fori_loop(0, width // CHUNK, step, 0)

    def by_eight(values):
        return values.reshape(CHUNK // 8, 8, values.shape[-1])

    def across(chunk):
        return by_eight(jnp.concatenate([tops[chunk, :]] * (rows * groups), axis=1))

    def fold(values, combine):
        lanes = [values[..., g * LANES : (g + 1) * LANES] for g in range(rows * groups)]
        return functools.reduce(combine, lanes).reshape(CHUNK, LANES)

    every = part1[...]
    top = jnp.max(every, axis=0)
    row_lse = top + jnp.log(jnp.sum(jnp.exp(every - top[None]), axis=0))
    weights = gathered(groups)
    row_pot = spread((weights - row_lse) - gathered(0))[None]
    mass = jnp.exp(weights) * float(width * cols)

    def largest(chunk):
        sums[chunk, :] = fold(by_eight(tile[chunk, :]) + row_pot, jnp.maximum)

    def entries(chunk):
        shifted = (by_eight(tile[chunk, :]) + row_pot) - across(chunk)
        values = jnp.exp(shifted)
        tile[chunk, :] = values.reshape(CHUNK, total)
        sums[chunk, :] = fold(values, jnp.add)

    def column_sums(factor):
        def body(chunk):
            sums[chunk, :] = fold(by_eight(tile[chunk, :]) * factor[None], jnp.add)

        sweep(body)

    def invert():
        inverse = 1.0 / jnp.sum(sums[...], axis=1, keepdims=True)
        tops[...] = jnp.broadcast_to(inverse, tops.shape)

    def row_sums(part):
        def step(index, acc):
            chunk = chunk_at(index)
            return acc + jnp.sum(by_eight(tile[chunk, :]) * across(chunk), axis=0)

        acc = lax.fori_loop(0, width // CHUNK, step, jnp.zeros((8, total), jnp.float32))
        summed = jnp.sum(acc, axis=0, keepdims=True)
        for g in range(rows * groups):
            part[0, g : g + 1, :] = summed[:, g * LANES : (g + 1) * LANES]

    def finish(copies, part):
        for copy in copies:
            copy.wait_recv()
        return spread(mass / jnp.sum(part[...], axis=0))

    sweep(largest)
    tops[...] = jnp.broadcast_to(jnp.max(sums[...], axis=1, keepdims=True), tops.shape)
    sweep(entries)
    invert()
    row_sums(part2)
    second = exchange(part2, 1)
    column_sums(finish(second, part2))
    invert()
    row_sums(part3)
    third = exchange(part3, 2)
    factor = finish(third, part3)

    share = width // rows
    mine = tile[pl.ds(pl.multiple_of(row * share, 8), share), :]
    mine = (mine.reshape(share // 8, 8, total) * factor[None]).reshape(share, total)
    plan = mine * (1.0 / jnp.sum(mine, axis=1, keepdims=True))
    out_ref[...] = jnp.dot(
        plan.astype(jnp.bfloat16), source_half[...], preferred_element_type=jnp.float32
    )

    for copy in far_copies + [pair_copy] + forwards + pot_copies + second + third:
        copy.wait_send()
    each_first(lambda copy: copy.wait_send())


def per_device_small(cols, particles, log_weights, targets):
    block, feature = particles.shape
    width = targets.shape[0]
    groups = block // LANES
    part = pltpu.VMEM((cols, 8, LANES), jnp.float32)
    hbm = pl.BlockSpec(memory_space=pltpu.HBM)
    vmem = pl.BlockSpec(memory_space=pltpu.VMEM)
    return pl.pallas_call(
        functools.partial(kernel, cols),
        out_shape=jax.ShapeDtypeStruct((width // 4, feature), jnp.float32),
        in_specs=[hbm, hbm, hbm],
        out_specs=vmem,
        scratch_shapes=[
            pltpu.VMEM((4, block, feature), jnp.float32),
            pltpu.VMEM((width, feature), jnp.float32),
            pltpu.VMEM((groups, LANES), jnp.float32),
            pltpu.VMEM((width, 6 * feature), jnp.bfloat16),
            pltpu.VMEM((4 * block, feature), jnp.bfloat16),
            pltpu.VMEM((width, 4 * block), jnp.float32),
            pltpu.VMEM((width, LANES), jnp.float32),
            pltpu.VMEM((width, LANES), jnp.float32),
            part,
            part,
            part,
            pltpu.VMEM((4, 8, LANES), jnp.float32),
            pltpu.SemaphoreType.DMA((3,)),
            pltpu.SemaphoreType.DMA((2, 1)),
            pltpu.SemaphoreType.DMA((2, PIECES)),
            pltpu.SemaphoreType.DMA((2, PIECES)),
            pltpu.SemaphoreType.DMA((2, 4)),
            pltpu.SemaphoreType.DMA((3, 2, cols)),
            pltpu.SemaphoreType.DMA((2, 4, cols)),
        ],
        compiler_params=pltpu.CompilerParams(
            collective_id=0, has_side_effects=True, vmem_limit_bytes=GRANT
        ),
    )(particles, log_weights.reshape(groups, LANES), targets)


def per_device(rows, cols, particles, log_weights, targets):
    block = particles.shape[0]
    width = targets.shape[0]
    if rows == 4 and block == 2 * LANES and width % CHUNK == 0 and width % 64 == 0 and width <= 1024:
        return per_device_small(cols, particles, log_weights, targets)
    return per_device_large(particles, log_weights, targets)


def solution(mesh):
    placed = (P("row", None), P("row"), P("col", None))
    return jax.shard_map(
        functools.partial(per_device, mesh.shape["row"], mesh.shape["col"]),
        mesh=mesh,
        in_specs=placed,
        out_specs=P(("col", "row"), None),
        check_vma=False,
    )
```

```python
import functools
import math

import jax
import jax.numpy as jnp
from jax import lax
from jax.experimental import pallas as pl
from jax.experimental.pallas import tpu as pltpu
from jax.sharding import PartitionSpec as P

ITERS = 3


EPS = 0.01
MESH = pl.DeviceIdType.MESH
HIGHEST = lax.Precision.HIGHEST
LANES = 128
CHUNK = 64
GRANT = 55168 * 1024
PIECES = 2


def cost_tile(source, points):
    source_sq = jnp.sum(source * source, axis=1)
    points_sq = jnp.sum(points * points, axis=1)
    cross = jnp.dot(source, points.T, precision=HIGHEST, preferred_element_type=jnp.float32)
    return (source_sq[:, None] + points_sq[None, :] - 2.0 * cross) / source.shape[1]


def row_update(particles, log_weights, targets, col_pot, block_count, block_rows):
    maxima = []
    totals = []
    for index in range(block_count):
        source = particles[index * block_rows : (index + 1) * block_rows]
        scores = (col_pot[None, :] - cost_tile(source, targets)) / EPS
        top = jnp.max(scores, axis=1)
        maxima.append(top)
        totals.append(jnp.sum(jnp.exp(scores - top[:, None]), axis=1))
    local_top = jnp.concatenate(maxima)
    local_sum = jnp.concatenate(totals)
    top = lax.pmax(local_top, "col")
    summed = lax.psum(local_sum * jnp.exp(local_top - top), "col")
    return EPS * (log_weights - (top + jnp.log(summed)))


def col_update(particles, targets, row_pot, block_count, block_rows):
    width = targets.shape[0]
    top = jnp.full((width,), -1e30, jnp.float32)
    summed = jnp.zeros((width,), jnp.float32)
    for index in range(block_count):
        source = particles[index * block_rows : (index + 1) * block_rows]
        potential = row_pot[index * block_rows : (index + 1) * block_rows]
        scores = (potential[:, None] - cost_tile(source, targets)) / EPS
        fresh = jnp.maximum(top, jnp.max(scores, axis=0))
        summed = summed * jnp.exp(top - fresh) + jnp.sum(jnp.exp(scores - fresh[None, :]), axis=0)
        top = fresh
    global_top = lax.pmax(top, "row")
    summed = lax.psum(summed * jnp.exp(top - global_top), "row")
    return global_top + jnp.log(summed)


def per_device_large(particles, log_weights, targets):
    row_count = particles.shape[0]
    block_count = max(1, row_count // 512)
    block_rows = row_count // block_count
    log_count = math.log(targets.shape[0] * lax.axis_size("col"))
    col_pot = jnp.zeros((targets.shape[0],), jnp.float32)
    col_lse = col_pot
    row_pot = log_weights
    for iteration in range(ITERS):
        row_pot = row_update(particles, log_weights, targets, col_pot, block_count, block_rows)
        col_lse = col_update(particles, targets, row_pot, block_count, block_rows)
        col_pot = EPS * (-log_count - col_lse)
    particles_half = particles.astype(jnp.bfloat16)
    acc = jnp.zeros(
        (lax.axis_size("row") * (targets.shape[0] // lax.axis_size("row")), particles.shape[1]),
        jnp.float32,
    )
    for index in range(block_count):
        source = particles[index * block_rows : (index + 1) * block_rows]
        potential = row_pot[index * block_rows : (index + 1) * block_rows]
        plan = jnp.exp(
            (potential[:, None] - cost_tile(source, targets)) / EPS - col_lse[None, :]
        ).astype(jnp.bfloat16)
        source_half = particles_half[index * block_rows : (index + 1) * block_rows]
        acc = acc + lax.dot_general(
            plan, source_half, (((0,), (0,)), ((), ())), preferred_element_type=jnp.float32
        )
    return lax.psum_scatter(acc, "row", scatter_dimension=0, tiled=True)


def dot_minor(a, b, precision):
    return lax.dot_general(
        a, b, (((1,), (1,)), ((), ())), precision=precision, preferred_element_type=jnp.float32
    )


def split(values):
    high = values.astype(jnp.bfloat16)
    rest = values - high.astype(jnp.float32)
    middle = rest.astype(jnp.bfloat16)
    low = (rest - middle.astype(jnp.float32)).astype(jnp.bfloat16)
    return high, middle, low


def kernel(
    cols,
    x_hbm,
    w_hbm,
    y_hbm,
    out_ref,
    held,
    points,
    weights_ref,
    point_parts,
    source_half,
    tile,
    sums,
    tops,
    part1,
    part2,
    part3,
    pots,
    local_sem,
    pair_sem,
    far_sem,
    fwd_sem,
    pot_sem,
    part_sem,
):
    rows = 4
    row = lax.axis_index("row")
    col = lax.axis_index("col")
    side = lax.rem(row, 2)
    twin = row + 1 - 2 * side
    far = lax.rem(row + 2, rows)
    far_twin = lax.rem(twin + 2, rows)
    block, feature = x_hbm.shape
    width = y_hbm.shape[0]
    total = rows * block
    groups = block // LANES
    piece = block // PIECES

    load_x = pltpu.make_async_copy(x_hbm, held.at[0], local_sem.at[0])
    load_y = pltpu.make_async_copy(y_hbm, points, local_sem.at[1])
    load_w = pltpu.make_async_copy(w_hbm, weights_ref, local_sem.at[2])
    load_y.start()
    load_x.start()
    load_w.start()

    barrier = pltpu.get_barrier_semaphore()
    for peer in (twin, far, far_twin):
        pl.semaphore_signal(barrier, inc=1, device_id=(peer, col), device_id_type=MESH)
    for step in range(1, cols):
        pl.semaphore_signal(
            barrier, inc=1, device_id=(row, lax.rem(col + step, cols)), device_id_type=MESH
        )

    def send(src, dst, sems, index, device):
        copy = pltpu.make_async_remote_copy(
            src_ref=src,
            dst_ref=dst,
            send_sem=sems.at[0, index],
            recv_sem=sems.at[1, index],
            device_id=device,
            device_id_type=MESH,
        )
        copy.start()
        return copy

    pl.semaphore_wait(barrier, rows - 1 + cols - 1)
    far_copies = []
    for index in range(PIECES):
        span = pl.ds(index * piece, piece)
        far_copies.append(send(x_hbm.at[span], held.at[2, span], far_sem, index, (far, col)))
    pair_copy = send(x_hbm, held.at[1], pair_sem, 0, (twin, col))

    scale = 2.0 / (feature * EPS)
    half = 1.0 / (feature * EPS)
    load_y.wait()
    y = points[...]
    y_square = jnp.sum(y * y, axis=1, keepdims=True) * half
    high, middle, low = split(y * scale)
    for place, part in enumerate((high, middle, high, middle)):
        point_parts[:, place * feature : (place + 1) * feature] = part

    def score(slot, start=0, size=block):
        high, middle, low = split(held[slot, start : start + size])
        first_lane = slot * block + start
        source_half[first_lane : first_lane + size, :] = high
        source_parts = jnp.concatenate([high, high, middle, middle], axis=1)
        cross = dot_minor(point_parts[...], source_parts, None)
        tile[:, first_lane : first_lane + size] = cross - y_square

    def exchange(part, index, size):
        copies = []
        for step in range(1, cols):
            copies.append(
                send(
                    part.at[0, :size],
                    part.at[step, :size],
                    part_sem.at[index],
                    step,
                    (row, lax.rem(col + step, cols)),
                )
            )
        return copies

    load_x.wait()
    load_w.wait()
    score(0)
    source = held[0]
    square_parts = jnp.concatenate(split(source * source), axis=1)
    square = dot_minor(jnp.ones((16, 3 * feature), jnp.bfloat16), square_parts, None)[:1] * half
    own = tile[:, :block] - square
    top = jnp.max(own, axis=0, keepdims=True)
    lse = top + jnp.log(jnp.sum(jnp.exp(own - top), axis=0, keepdims=True))
    for group in range(groups):
        part1[0, group : group + 1, :] = lse[:, group * LANES : (group + 1) * LANES]

    first = exchange(part1, 0, groups)

    pair_copy.wait_recv()
    score(1)
    forwards = []
    for index in range(PIECES):
        far_copies[index].wait_recv()
        span = pl.ds(index * piece, piece)
        forwards.append(send(held.at[2, span], held.at[3, span], fwd_sem, index, (twin, col)))
        if index == 0:
            for copy in first:
                copy.wait_recv()
            every = part1[:, :groups, :]
            top = jnp.max(every, axis=0)
            row_lse = top + jnp.log(jnp.sum(jnp.exp(every - top[None]), axis=0))
            weights = weights_ref[...]
            for group in range(groups):
                pots[0, group : group + 1, :] = (weights - row_lse)[group : group + 1] - square[
                    :, group * LANES : (group + 1) * LANES
                ]
            pots[0, groups : 2 * groups, :] = weights
            used = 2 * groups
            pot_copies = [
                send(pots.at[0, :used], pots.at[slot, :used], pot_sem, slot, (peer, col))
                for slot, peer in ((1, twin), (2, far), (3, far_twin))
            ]
        score(2, index * piece, piece)
    for index in range(PIECES):
        forwards[index].wait_recv()
        score(3, index * piece, piece)
    for copy in pot_copies:
        copy.wait_recv()

    def spread(compact):
        return jnp.concatenate(
            [jnp.broadcast_to(compact[g : g + 1, :], (8, LANES)) for g in range(rows * groups)],
            axis=1,
        )

    def gathered(first_row):
        return jnp.concatenate(
            [pots[slot, first_row : first_row + groups, :] for slot in range(rows)], axis=0
        )

    def chunk_at(index):
        return pl.ds(pl.multiple_of(index * CHUNK, CHUNK), CHUNK)

    def sweep(body):
        def step(index, carry):
            body(chunk_at(index))
            return carry

        lax.fori_loop(0, width // CHUNK, step, 0, unroll=True)

    def by_eight(values):
        return values.reshape(CHUNK // 8, 8, values.shape[-1])

    def across(chunk):
        return by_eight(jnp.concatenate([tops[chunk, :]] * (rows * groups), axis=1))

    def fold(values, combine):
        lanes = [values[..., g * LANES : (g + 1) * LANES] for g in range(rows * groups)]
        return functools.reduce(combine, lanes).reshape(CHUNK, LANES)

    row_pot = spread(gathered(0))[None]
    mass = jnp.exp(gathered(groups)) * float(width * cols)

    def largest(chunk):
        sums[chunk, :] = fold(by_eight(tile[chunk, :]) + row_pot, jnp.maximum)

    def entries(chunk):
        shifted = (by_eight(tile[chunk, :]) + row_pot) - across(chunk)
        values = jnp.exp(shifted)
        tile[chunk, :] = values.reshape(CHUNK, total)
        sums[chunk, :] = fold(values, jnp.add)

    def column_sums(factor):
        def body(chunk):
            sums[chunk, :] = fold(by_eight(tile[chunk, :]) * factor[None], jnp.add)

        sweep(body)

    def invert():
        inverse = 1.0 / jnp.sum(sums[...], axis=1, keepdims=True)
        tops[...] = jnp.broadcast_to(inverse, tops.shape)

    def row_sums(part):
        def step(index, acc):
            chunk = chunk_at(index)
            return acc + jnp.sum(by_eight(tile[chunk, :]) * across(chunk), axis=0)

        acc = lax.fori_loop(
            0, width // CHUNK, step, jnp.zeros((8, total), jnp.float32), unroll=True
        )
        summed = jnp.sum(acc, axis=0, keepdims=True)
        for g in range(rows * groups):
            part[0, g : g + 1, :] = summed[:, g * LANES : (g + 1) * LANES]

    def finish(copies, part):
        for copy in copies:
            copy.wait_recv()
        return spread(mass / jnp.sum(part[...], axis=0))

    sweep(largest)
    tops[...] = jnp.broadcast_to(jnp.max(sums[...], axis=1, keepdims=True), tops.shape)
    sweep(entries)
    invert()
    row_sums(part2)
    second = exchange(part2, 1, rows * groups)
    column_sums(finish(second, part2))
    invert()
    row_sums(part3)
    third = exchange(part3, 2, rows * groups)
    factor = finish(third, part3)

    share = width // rows
    mine = tile[pl.ds(pl.multiple_of(row * share, 8), share), :]
    mine = (mine.reshape(share // 8, 8, total) * factor[None]).reshape(share, total)
    plan = mine * (1.0 / jnp.sum(mine, axis=1, keepdims=True))
    out_ref[...] = jnp.dot(
        plan.astype(jnp.bfloat16), source_half[...], preferred_element_type=jnp.float32
    )

    for copy in far_copies + [pair_copy] + forwards + pot_copies + first + second + third:
        copy.wait_send()


def per_device_small(cols, particles, log_weights, targets):
    block, feature = particles.shape
    width = targets.shape[0]
    groups = block // LANES
    part = pltpu.VMEM((cols, 8, LANES), jnp.float32)
    hbm = pl.BlockSpec(memory_space=pltpu.HBM)
    vmem = pl.BlockSpec(memory_space=pltpu.VMEM)
    return pl.pallas_call(
        functools.partial(kernel, cols),
        out_shape=jax.ShapeDtypeStruct((width // 4, feature), jnp.float32),
        in_specs=[hbm, hbm, hbm],
        out_specs=vmem,
        scratch_shapes=[
            pltpu.VMEM((4, block, feature), jnp.float32),
            pltpu.VMEM((width, feature), jnp.float32),
            pltpu.VMEM((groups, LANES), jnp.float32),
            pltpu.VMEM((width, 4 * feature), jnp.bfloat16),
            pltpu.VMEM((4 * block, feature), jnp.bfloat16),
            pltpu.VMEM((width, 4 * block), jnp.float32),
            pltpu.VMEM((width, LANES), jnp.float32),
            pltpu.VMEM((width, LANES), jnp.float32),
            part,
            part,
            part,
            pltpu.VMEM((4, 8, LANES), jnp.float32),
            pltpu.SemaphoreType.DMA((3,)),
            pltpu.SemaphoreType.DMA((2, 1)),
            pltpu.SemaphoreType.DMA((2, PIECES)),
            pltpu.SemaphoreType.DMA((2, PIECES)),
            pltpu.SemaphoreType.DMA((2, 4)),
            pltpu.SemaphoreType.DMA((3, 2, cols)),
        ],
        compiler_params=pltpu.CompilerParams(
            collective_id=0, has_side_effects=True, vmem_limit_bytes=GRANT
        ),
    )(particles, log_weights.reshape(groups, LANES), targets)


def per_device(rows, cols, particles, log_weights, targets):
    block = particles.shape[0]
    width = targets.shape[0]
    if rows == 4 and block == 2 * LANES and width % CHUNK == 0 and width % 64 == 0 and width <= 1024:
        return per_device_small(cols, particles, log_weights, targets)
    return per_device_large(particles, log_weights, targets)


def solution(mesh):
    placed = (P("row", None), P("row"), P("col", None))
    return jax.shard_map(
        functools.partial(per_device, mesh.shape["row"], mesh.shape["col"]),
        mesh=mesh,
        in_specs=placed,
        out_specs=P(("col", "row"), None),
        check_vma=False,
    )
```

```python
import functools
import math

import jax
import jax.numpy as jnp
from jax import lax
from jax.experimental import pallas as pl
from jax.experimental.pallas import tpu as pltpu
from jax.sharding import PartitionSpec as P

ITERS = 3


EPS = 0.01
MESH = pl.DeviceIdType.MESH
HIGHEST = lax.Precision.HIGHEST
LANES = 128
CHUNK = 64
GRANT = 55168 * 1024
PIECES = 2


def cost_tile(source, points):
    source_sq = jnp.sum(source * source, axis=1)
    points_sq = jnp.sum(points * points, axis=1)
    cross = jnp.dot(source, points.T, precision=HIGHEST, preferred_element_type=jnp.float32)
    return (source_sq[:, None] + points_sq[None, :] - 2.0 * cross) / source.shape[1]


def row_update(particles, log_weights, targets, col_pot, block_count, block_rows):
    maxima = []
    totals = []
    for index in range(block_count):
        source = particles[index * block_rows : (index + 1) * block_rows]
        scores = (col_pot[None, :] - cost_tile(source, targets)) / EPS
        top = jnp.max(scores, axis=1)
        maxima.append(top)
        totals.append(jnp.sum(jnp.exp(scores - top[:, None]), axis=1))
    local_top = jnp.concatenate(maxima)
    local_sum = jnp.concatenate(totals)
    top = lax.pmax(local_top, "col")
    summed = lax.psum(local_sum * jnp.exp(local_top - top), "col")
    return EPS * (log_weights - (top + jnp.log(summed)))


def col_update(particles, targets, row_pot, block_count, block_rows):
    width = targets.shape[0]
    top = jnp.full((width,), -1e30, jnp.float32)
    summed = jnp.zeros((width,), jnp.float32)
    for index in range(block_count):
        source = particles[index * block_rows : (index + 1) * block_rows]
        potential = row_pot[index * block_rows : (index + 1) * block_rows]
        scores = (potential[:, None] - cost_tile(source, targets)) / EPS
        fresh = jnp.maximum(top, jnp.max(scores, axis=0))
        summed = summed * jnp.exp(top - fresh) + jnp.sum(jnp.exp(scores - fresh[None, :]), axis=0)
        top = fresh
    global_top = lax.pmax(top, "row")
    summed = lax.psum(summed * jnp.exp(top - global_top), "row")
    return global_top + jnp.log(summed)


def per_device_large(particles, log_weights, targets):
    row_count = particles.shape[0]
    block_count = max(1, row_count // 512)
    block_rows = row_count // block_count
    log_count = math.log(targets.shape[0] * lax.axis_size("col"))
    col_pot = jnp.zeros((targets.shape[0],), jnp.float32)
    col_lse = col_pot
    row_pot = log_weights
    for iteration in range(ITERS):
        row_pot = row_update(particles, log_weights, targets, col_pot, block_count, block_rows)
        col_lse = col_update(particles, targets, row_pot, block_count, block_rows)
        col_pot = EPS * (-log_count - col_lse)
    particles_half = particles.astype(jnp.bfloat16)
    acc = jnp.zeros(
        (lax.axis_size("row") * (targets.shape[0] // lax.axis_size("row")), particles.shape[1]),
        jnp.float32,
    )
    for index in range(block_count):
        source = particles[index * block_rows : (index + 1) * block_rows]
        potential = row_pot[index * block_rows : (index + 1) * block_rows]
        plan = jnp.exp(
            (potential[:, None] - cost_tile(source, targets)) / EPS - col_lse[None, :]
        ).astype(jnp.bfloat16)
        source_half = particles_half[index * block_rows : (index + 1) * block_rows]
        acc = acc + lax.dot_general(
            plan, source_half, (((0,), (0,)), ((), ())), preferred_element_type=jnp.float32
        )
    return lax.psum_scatter(acc, "row", scatter_dimension=0, tiled=True)


def dot_minor(a, b, precision):
    return lax.dot_general(
        a, b, (((1,), (1,)), ((), ())), precision=precision, preferred_element_type=jnp.float32
    )


def split(values):
    high = values.astype(jnp.bfloat16)
    rest = values - high.astype(jnp.float32)
    middle = rest.astype(jnp.bfloat16)
    low = (rest - middle.astype(jnp.float32)).astype(jnp.bfloat16)
    return high, middle, low


def kernel(
    cols,
    x_hbm,
    w_hbm,
    y_hbm,
    out_ref,
    held,
    points,
    weights_ref,
    point_parts,
    source_half,
    tile,
    sums,
    tops,
    part1,
    part2,
    part3,
    pots,
    local_sem,
    pair_sem,
    far_sem,
    fwd_sem,
    pot_sem,
    part_sem,
):
    rows = 4
    row = lax.axis_index("row")
    col = lax.axis_index("col")
    side = lax.rem(row, 2)
    twin = row + 1 - 2 * side
    far = lax.rem(row + 2, rows)
    far_twin = lax.rem(twin + 2, rows)
    block, feature = x_hbm.shape
    width = y_hbm.shape[0]
    total = rows * block
    groups = block // LANES
    piece = block // PIECES

    load_x = pltpu.make_async_copy(x_hbm, held.at[0], local_sem.at[0])
    load_y = pltpu.make_async_copy(y_hbm, points, local_sem.at[1])
    load_w = pltpu.make_async_copy(w_hbm, weights_ref, local_sem.at[2])
    load_y.start()
    load_x.start()
    load_w.start()

    barrier = pltpu.get_barrier_semaphore()
    for peer in (twin, far, far_twin):
        pl.semaphore_signal(barrier, inc=1, device_id=(peer, col), device_id_type=MESH)
    for step in range(1, cols):
        pl.semaphore_signal(
            barrier, inc=1, device_id=(row, lax.rem(col + step, cols)), device_id_type=MESH
        )

    def send(src, dst, sems, index, device):
        copy = pltpu.make_async_remote_copy(
            src_ref=src,
            dst_ref=dst,
            send_sem=sems.at[0, index],
            recv_sem=sems.at[1, index],
            device_id=device,
            device_id_type=MESH,
        )
        copy.start()
        return copy

    pl.semaphore_wait(barrier, rows - 1 + cols - 1)
    far_copies = []
    for index in range(PIECES):
        span = pl.ds(index * piece, piece)
        far_copies.append(send(x_hbm.at[span], held.at[2, span], far_sem, index, (far, col)))
    pair_copy = send(x_hbm, held.at[1], pair_sem, 0, (twin, col))

    scale = 2.0 / (feature * EPS)
    half = 1.0 / (feature * EPS)
    load_y.wait()
    y = points[...]
    y_square = jnp.sum(y * y, axis=1, keepdims=True) * half
    high, middle, low = split(y * scale)
    for place, part in enumerate((high, middle, high, middle)):
        point_parts[:, place * feature : (place + 1) * feature] = part

    def score(slot, start=0, size=block):
        high, middle, low = split(held[slot, start : start + size])
        first_lane = slot * block + start
        source_half[first_lane : first_lane + size, :] = high
        source_parts = jnp.concatenate([high, high, middle, middle], axis=1)
        cross = dot_minor(point_parts[...], source_parts, None)
        tile[:, first_lane : first_lane + size] = cross - y_square

    def exchange(part, index, size):
        copies = []
        for step in range(1, cols):
            copies.append(
                send(
                    part.at[0, :size],
                    part.at[step, :size],
                    part_sem.at[index],
                    step,
                    (row, lax.rem(col + step, cols)),
                )
            )
        return copies

    load_x.wait()
    load_w.wait()
    score(0)
    source = held[0]
    square_parts = jnp.concatenate(split(source * source), axis=1)
    square = dot_minor(jnp.ones((16, 3 * feature), jnp.bfloat16), square_parts, None)[:1] * half
    own = tile[:, :block]
    top = jnp.max(own, axis=0, keepdims=True)
    lse = top + jnp.log(jnp.sum(jnp.exp(own - top), axis=0, keepdims=True)) - square
    for group in range(groups):
        part1[0, group : group + 1, :] = lse[:, group * LANES : (group + 1) * LANES]

    first = exchange(part1, 0, groups)

    pair_copy.wait_recv()
    score(1)
    forwards = []
    for index in range(PIECES):
        far_copies[index].wait_recv()
        span = pl.ds(index * piece, piece)
        forwards.append(send(held.at[2, span], held.at[3, span], fwd_sem, index, (twin, col)))
        if index == 0:
            for copy in first:
                copy.wait_recv()
            every = part1[:, :groups, :]
            top = jnp.max(every, axis=0)
            row_lse = top + jnp.log(jnp.sum(jnp.exp(every - top[None]), axis=0))
            weights = weights_ref[...]
            for group in range(groups):
                pots[0, group : group + 1, :] = (weights - row_lse)[group : group + 1] - square[
                    :, group * LANES : (group + 1) * LANES
                ]
            pots[0, groups : 2 * groups, :] = weights
            used = 2 * groups
            pot_copies = [
                send(pots.at[0, :used], pots.at[slot, :used], pot_sem, slot, (peer, col))
                for slot, peer in ((1, twin), (2, far), (3, far_twin))
            ]
    score(2)
    for index in range(PIECES):
        forwards[index].wait_recv()
    score(3)
    for copy in pot_copies:
        copy.wait_recv()

    def spread(compact):
        return jnp.concatenate(
            [jnp.broadcast_to(compact[g : g + 1, :], (8, LANES)) for g in range(rows * groups)],
            axis=1,
        )

    def gathered(first_row):
        return jnp.concatenate(
            [pots[slot, first_row : first_row + groups, :] for slot in range(rows)], axis=0
        )

    def chunk_at(index):
        return pl.ds(pl.multiple_of(index * CHUNK, CHUNK), CHUNK)

    def sweep(body):
        def step(index, carry):
            body(chunk_at(index))
            return carry

        lax.fori_loop(0, width // CHUNK, step, 0, unroll=True)

    def by_eight(values):
        return values.reshape(CHUNK // 8, 8, values.shape[-1])

    def across(chunk):
        return by_eight(jnp.concatenate([tops[chunk, :]] * (rows * groups), axis=1))

    def fold(values, combine):
        lanes = [values[..., g * LANES : (g + 1) * LANES] for g in range(rows * groups)]
        return functools.reduce(combine, lanes).reshape(CHUNK, LANES)

    row_pot = spread(gathered(0))[None]
    mass = jnp.exp(gathered(groups)) * float(width * cols)

    def largest(chunk):
        sums[chunk, :] = fold(by_eight(tile[chunk, :]) + row_pot, jnp.maximum)

    def entries(chunk):
        shifted = (by_eight(tile[chunk, :]) + row_pot) - across(chunk)
        values = jnp.exp(shifted)
        tile[chunk, :] = values.reshape(CHUNK, total)
        sums[chunk, :] = fold(values, jnp.add)

    def column_sums(factor):
        def body(chunk):
            sums[chunk, :] = fold(by_eight(tile[chunk, :]) * factor[None], jnp.add)

        sweep(body)

    def invert():
        inverse = 1.0 / jnp.sum(sums[...], axis=1, keepdims=True)
        tops[...] = jnp.broadcast_to(inverse, tops.shape)

    def row_sums(part):
        def step(index, acc):
            chunk = chunk_at(index)
            return acc + jnp.sum(by_eight(tile[chunk, :]) * across(chunk), axis=0)

        acc = lax.fori_loop(
            0, width // CHUNK, step, jnp.zeros((8, total), jnp.float32), unroll=True
        )
        summed = jnp.sum(acc, axis=0, keepdims=True)
        for g in range(rows * groups):
            part[0, g : g + 1, :] = summed[:, g * LANES : (g + 1) * LANES]

    def finish(copies, part):
        for copy in copies:
            copy.wait_recv()
        return spread(mass / jnp.sum(part[...], axis=0))

    sweep(largest)
    tops[...] = jnp.broadcast_to(jnp.max(sums[...], axis=1, keepdims=True), tops.shape)
    sweep(entries)
    invert()
    row_sums(part2)
    second = exchange(part2, 1, rows * groups)
    column_sums(finish(second, part2))
    invert()
    row_sums(part3)
    third = exchange(part3, 2, rows * groups)
    factor = finish(third, part3)

    share = width // rows
    mine = tile[pl.ds(pl.multiple_of(row * share, 8), share), :]
    mine = (mine.reshape(share // 8, 8, total) * factor[None]).reshape(share, total)
    plan = mine * (1.0 / jnp.sum(mine, axis=1, keepdims=True))
    out_ref[...] = jnp.dot(
        plan.astype(jnp.bfloat16), source_half[...], preferred_element_type=jnp.float32
    )

    for copy in far_copies + [pair_copy] + forwards + pot_copies + first + second + third:
        copy.wait_send()


def per_device_small(cols, particles, log_weights, targets):
    block, feature = particles.shape
    width = targets.shape[0]
    groups = block // LANES
    part = pltpu.VMEM((cols, 8, LANES), jnp.float32)
    hbm = pl.BlockSpec(memory_space=pltpu.HBM)
    vmem = pl.BlockSpec(memory_space=pltpu.VMEM)
    return pl.pallas_call(
        functools.partial(kernel, cols),
        out_shape=jax.ShapeDtypeStruct((width // 4, feature), jnp.float32),
        in_specs=[hbm, hbm, hbm],
        out_specs=vmem,
        scratch_shapes=[
            pltpu.VMEM((4, block, feature), jnp.float32),
            pltpu.VMEM((width, feature), jnp.float32),
            pltpu.VMEM((groups, LANES), jnp.float32),
            pltpu.VMEM((width, 4 * feature), jnp.bfloat16),
            pltpu.VMEM((4 * block, feature), jnp.bfloat16),
            pltpu.VMEM((width, 4 * block), jnp.float32),
            pltpu.VMEM((width, LANES), jnp.float32),
            pltpu.VMEM((width, LANES), jnp.float32),
            part,
            part,
            part,
            pltpu.VMEM((4, 8, LANES), jnp.float32),
            pltpu.SemaphoreType.DMA((3,)),
            pltpu.SemaphoreType.DMA((2, 1)),
            pltpu.SemaphoreType.DMA((2, PIECES)),
            pltpu.SemaphoreType.DMA((2, PIECES)),
            pltpu.SemaphoreType.DMA((2, 4)),
            pltpu.SemaphoreType.DMA((3, 2, cols)),
        ],
        compiler_params=pltpu.CompilerParams(
            collective_id=0, has_side_effects=True, vmem_limit_bytes=GRANT
        ),
    )(particles, log_weights.reshape(groups, LANES), targets)


def per_device(rows, cols, particles, log_weights, targets):
    block = particles.shape[0]
    width = targets.shape[0]
    if rows == 4 and block == 2 * LANES and width % CHUNK == 0 and width % 64 == 0 and width <= 1024:
        return per_device_small(cols, particles, log_weights, targets)
    return per_device_large(particles, log_weights, targets)


def solution(mesh):
    placed = (P("row", None), P("row"), P("col", None))
    return jax.shard_map(
        functools.partial(per_device, mesh.shape["row"], mesh.shape["col"]),
        mesh=mesh,
        in_specs=placed,
        out_specs=P(("col", "row"), None),
        check_vma=False,
    )
```

```python
import functools
import math

import jax
import jax.numpy as jnp
from jax import lax
from jax.experimental import pallas as pl
from jax.experimental.pallas import tpu as pltpu
from jax.sharding import PartitionSpec as P

ITERS = 3


EPS = 0.01
MESH = pl.DeviceIdType.MESH
HIGHEST = lax.Precision.HIGHEST
LANES = 128
CHUNK = 64
GRANT = 55168 * 1024
PIECES = 2


def cost_tile(source, points):
    source_sq = jnp.sum(source * source, axis=1)
    points_sq = jnp.sum(points * points, axis=1)
    cross = jnp.dot(source, points.T, precision=HIGHEST, preferred_element_type=jnp.float32)
    return (source_sq[:, None] + points_sq[None, :] - 2.0 * cross) / source.shape[1]


def row_update(particles, log_weights, targets, col_pot, block_count, block_rows):
    maxima = []
    totals = []
    for index in range(block_count):
        source = particles[index * block_rows : (index + 1) * block_rows]
        scores = (col_pot[None, :] - cost_tile(source, targets)) / EPS
        top = jnp.max(scores, axis=1)
        maxima.append(top)
        totals.append(jnp.sum(jnp.exp(scores - top[:, None]), axis=1))
    local_top = jnp.concatenate(maxima)
    local_sum = jnp.concatenate(totals)
    top = lax.pmax(local_top, "col")
    summed = lax.psum(local_sum * jnp.exp(local_top - top), "col")
    return EPS * (log_weights - (top + jnp.log(summed)))


def col_update(particles, targets, row_pot, block_count, block_rows):
    width = targets.shape[0]
    top = jnp.full((width,), -1e30, jnp.float32)
    summed = jnp.zeros((width,), jnp.float32)
    for index in range(block_count):
        source = particles[index * block_rows : (index + 1) * block_rows]
        potential = row_pot[index * block_rows : (index + 1) * block_rows]
        scores = (potential[:, None] - cost_tile(source, targets)) / EPS
        fresh = jnp.maximum(top, jnp.max(scores, axis=0))
        summed = summed * jnp.exp(top - fresh) + jnp.sum(jnp.exp(scores - fresh[None, :]), axis=0)
        top = fresh
    global_top = lax.pmax(top, "row")
    summed = lax.psum(summed * jnp.exp(top - global_top), "row")
    return global_top + jnp.log(summed)


def per_device_large(particles, log_weights, targets):
    row_count = particles.shape[0]
    block_count = max(1, row_count // 512)
    block_rows = row_count // block_count
    log_count = math.log(targets.shape[0] * lax.axis_size("col"))
    col_pot = jnp.zeros((targets.shape[0],), jnp.float32)
    col_lse = col_pot
    row_pot = log_weights
    for iteration in range(ITERS):
        row_pot = row_update(particles, log_weights, targets, col_pot, block_count, block_rows)
        col_lse = col_update(particles, targets, row_pot, block_count, block_rows)
        col_pot = EPS * (-log_count - col_lse)
    particles_half = particles.astype(jnp.bfloat16)
    acc = jnp.zeros(
        (lax.axis_size("row") * (targets.shape[0] // lax.axis_size("row")), particles.shape[1]),
        jnp.float32,
    )
    for index in range(block_count):
        source = particles[index * block_rows : (index + 1) * block_rows]
        potential = row_pot[index * block_rows : (index + 1) * block_rows]
        plan = jnp.exp(
            (potential[:, None] - cost_tile(source, targets)) / EPS - col_lse[None, :]
        ).astype(jnp.bfloat16)
        source_half = particles_half[index * block_rows : (index + 1) * block_rows]
        acc = acc + lax.dot_general(
            plan, source_half, (((0,), (0,)), ((), ())), preferred_element_type=jnp.float32
        )
    return lax.psum_scatter(acc, "row", scatter_dimension=0, tiled=True)


def dot_minor(a, b, precision):
    return lax.dot_general(
        a, b, (((1,), (1,)), ((), ())), precision=precision, preferred_element_type=jnp.float32
    )


def split(values):
    high = values.astype(jnp.bfloat16)
    rest = values - high.astype(jnp.float32)
    middle = rest.astype(jnp.bfloat16)
    low = (rest - middle.astype(jnp.float32)).astype(jnp.bfloat16)
    return high, middle, low


def kernel(
    cols,
    x_hbm,
    w_hbm,
    y_hbm,
    out_ref,
    held,
    points,
    weights_ref,
    point_parts,
    source_half,
    tile,
    sums,
    part1,
    part2,
    part3,
    pots,
    local_sem,
    pair_sem,
    far_sem,
    fwd_sem,
    pot_sem,
    part_sem,
):
    rows = 4
    row = lax.axis_index("row")
    col = lax.axis_index("col")
    side = lax.rem(row, 2)
    twin = row + 1 - 2 * side
    far = lax.rem(row + 2, rows)
    far_twin = lax.rem(twin + 2, rows)
    block, feature = x_hbm.shape
    width = y_hbm.shape[0]
    total = rows * block
    groups = block // LANES
    piece = block // PIECES

    load_x = pltpu.make_async_copy(x_hbm, held.at[0], local_sem.at[0])
    load_y = pltpu.make_async_copy(y_hbm, points, local_sem.at[1])
    load_w = pltpu.make_async_copy(w_hbm, weights_ref, local_sem.at[2])
    load_y.start()
    load_x.start()
    load_w.start()

    barrier = pltpu.get_barrier_semaphore()
    for peer in (twin, far, far_twin):
        pl.semaphore_signal(barrier, inc=1, device_id=(peer, col), device_id_type=MESH)
    for step in range(1, cols):
        pl.semaphore_signal(
            barrier, inc=1, device_id=(row, lax.rem(col + step, cols)), device_id_type=MESH
        )

    def send(src, dst, sems, index, device):
        copy = pltpu.make_async_remote_copy(
            src_ref=src,
            dst_ref=dst,
            send_sem=sems.at[0, index],
            recv_sem=sems.at[1, index],
            device_id=device,
            device_id_type=MESH,
        )
        copy.start()
        return copy

    pl.semaphore_wait(barrier, rows - 1 + cols - 1)
    far_copies = []
    for index in range(PIECES):
        span = pl.ds(index * piece, piece)
        far_copies.append(send(x_hbm.at[span], held.at[2, span], far_sem, index, (far, col)))
    pair_copy = send(x_hbm, held.at[1], pair_sem, 0, (twin, col))

    scale = 2.0 / (feature * EPS)
    half = 1.0 / (feature * EPS)
    load_y.wait()
    y = points[...]
    y_square = jnp.sum(y * y, axis=1, keepdims=True) * half
    high, middle, low = split(y * scale)
    for place, part in enumerate((high, middle, high, middle)):
        point_parts[:, place * feature : (place + 1) * feature] = part

    def score(slot, start=0, size=block):
        high, middle, low = split(held[slot, start : start + size])
        first_lane = slot * block + start
        source_half[first_lane : first_lane + size, :] = high
        source_parts = jnp.concatenate([high, high, middle, middle], axis=1)
        cross = dot_minor(point_parts[...], source_parts, None)
        tile[:, first_lane : first_lane + size] = cross - y_square

    def exchange(part, index, size):
        copies = []
        for step in range(1, cols):
            copies.append(
                send(
                    part.at[0, :size],
                    part.at[step, :size],
                    part_sem.at[index],
                    step,
                    (row, lax.rem(col + step, cols)),
                )
            )
        return copies

    load_x.wait()
    load_w.wait()
    score(0)
    source = held[0]
    square_parts = jnp.concatenate(split(source * source), axis=1)
    square = dot_minor(jnp.ones((16, 3 * feature), jnp.bfloat16), square_parts, None)[:1] * half
    own = tile[:, :block]
    top = jnp.max(own, axis=0, keepdims=True)
    lse = top + jnp.log(jnp.sum(jnp.exp(own - top), axis=0, keepdims=True)) - square
    for group in range(groups):
        part1[0, group : group + 1, :] = lse[:, group * LANES : (group + 1) * LANES]

    first = exchange(part1, 0, groups)

    pair_copy.wait_recv()
    score(1)
    forwards = []
    for index in range(PIECES):
        far_copies[index].wait_recv()
        span = pl.ds(index * piece, piece)
        forwards.append(send(held.at[2, span], held.at[3, span], fwd_sem, index, (twin, col)))
        if index == 0:
            for copy in first:
                copy.wait_recv()
            every = part1[:, :groups, :]
            top = jnp.max(every, axis=0)
            row_lse = top + jnp.log(jnp.sum(jnp.exp(every - top[None]), axis=0))
            weights = weights_ref[...]
            for group in range(groups):
                pots[0, group : group + 1, :] = (weights - row_lse)[group : group + 1] - square[
                    :, group * LANES : (group + 1) * LANES
                ]
            pots[0, groups : 2 * groups, :] = weights
            used = 2 * groups
            pot_copies = [
                send(pots.at[0, :used], pots.at[slot, :used], pot_sem, slot, (peer, col))
                for slot, peer in ((1, twin), (2, far), (3, far_twin))
            ]
    score(2)
    for index in range(PIECES):
        forwards[index].wait_recv()
    score(3)
    for copy in pot_copies:
        copy.wait_recv()

    def spread(compact):
        return jnp.concatenate(
            [jnp.broadcast_to(compact[g : g + 1, :], (8, LANES)) for g in range(rows * groups)],
            axis=1,
        )

    def gathered(first_row):
        return jnp.concatenate(
            [pots[slot, first_row : first_row + groups, :] for slot in range(rows)], axis=0
        )

    def chunk_at(index):
        return pl.ds(pl.multiple_of(index * CHUNK, CHUNK), CHUNK)

    def sweep(body):
        def step(index, carry):
            body(chunk_at(index))
            return carry

        lax.fori_loop(0, width // CHUNK, step, 0, unroll=True)

    def by_eight(values):
        return values.reshape(CHUNK // 8, 8, values.shape[-1])

    def across(column):
        return by_eight(jnp.broadcast_to(column, (CHUNK, total)))

    def fold(values, combine):
        lanes = [values[..., g * LANES : (g + 1) * LANES] for g in range(rows * groups)]
        return functools.reduce(combine, lanes).reshape(CHUNK, LANES)

    row_pot = spread(gathered(0))[None]
    mass = jnp.exp(gathered(groups)) * float(width * cols)

    def largest(chunk):
        sums[chunk, :] = fold(by_eight(tile[chunk, :]) + row_pot, jnp.maximum)

    def entries(chunk):
        top = jnp.max(sums[chunk, :], axis=1, keepdims=True)
        shifted = (by_eight(tile[chunk, :]) + row_pot) - across(top)
        values = jnp.exp(shifted)
        tile[chunk, :] = values.reshape(CHUNK, total)
        sums[chunk, :] = fold(values, jnp.add)

    def column_sums(factor):
        def body(chunk):
            sums[chunk, :] = fold(by_eight(tile[chunk, :]) * factor[None], jnp.add)

        sweep(body)

    def row_sums(part):
        def step(index, acc):
            chunk = chunk_at(index)
            inverse = 1.0 / jnp.sum(sums[chunk, :], axis=1, keepdims=True)
            return acc + jnp.sum(by_eight(tile[chunk, :]) * across(inverse), axis=0)

        acc = lax.fori_loop(
            0, width // CHUNK, step, jnp.zeros((8, total), jnp.float32), unroll=True
        )
        summed = jnp.sum(acc, axis=0, keepdims=True)
        for g in range(rows * groups):
            part[0, g : g + 1, :] = summed[:, g * LANES : (g + 1) * LANES]

    def finish(copies, part):
        for copy in copies:
            copy.wait_recv()
        return spread(mass / jnp.sum(part[...], axis=0))

    sweep(largest)
    sweep(entries)
    row_sums(part2)
    second = exchange(part2, 1, rows * groups)
    column_sums(finish(second, part2))
    row_sums(part3)
    third = exchange(part3, 2, rows * groups)
    factor = finish(third, part3)

    share = width // rows
    mine = tile[pl.ds(pl.multiple_of(row * share, 8), share), :]
    mine = (mine.reshape(share // 8, 8, total) * factor[None]).reshape(share, total)
    plan = mine * (1.0 / jnp.sum(mine, axis=1, keepdims=True))
    out_ref[...] = jnp.dot(
        plan.astype(jnp.bfloat16), source_half[...], preferred_element_type=jnp.float32
    )

    for copy in far_copies + [pair_copy] + forwards + pot_copies + first + second + third:
        copy.wait_send()


def per_device_small(cols, particles, log_weights, targets):
    block, feature = particles.shape
    width = targets.shape[0]
    groups = block // LANES
    part = pltpu.VMEM((cols, 8, LANES), jnp.float32)
    hbm = pl.BlockSpec(memory_space=pltpu.HBM)
    vmem = pl.BlockSpec(memory_space=pltpu.VMEM)
    return pl.pallas_call(
        functools.partial(kernel, cols),
        out_shape=jax.ShapeDtypeStruct((width // 4, feature), jnp.float32),
        in_specs=[hbm, hbm, hbm],
        out_specs=vmem,
        scratch_shapes=[
            pltpu.VMEM((4, block, feature), jnp.float32),
            pltpu.VMEM((width, feature), jnp.float32),
            pltpu.VMEM((groups, LANES), jnp.float32),
            pltpu.VMEM((width, 4 * feature), jnp.bfloat16),
            pltpu.VMEM((4 * block, feature), jnp.bfloat16),
            pltpu.VMEM((width, 4 * block), jnp.float32),
            pltpu.VMEM((width, LANES), jnp.float32),
            part,
            part,
            part,
            pltpu.VMEM((4, 8, LANES), jnp.float32),
            pltpu.SemaphoreType.DMA((3,)),
            pltpu.SemaphoreType.DMA((2, 1)),
            pltpu.SemaphoreType.DMA((2, PIECES)),
            pltpu.SemaphoreType.DMA((2, PIECES)),
            pltpu.SemaphoreType.DMA((2, 4)),
            pltpu.SemaphoreType.DMA((3, 2, cols)),
        ],
        compiler_params=pltpu.CompilerParams(
            collective_id=0, has_side_effects=True, vmem_limit_bytes=GRANT
        ),
    )(particles, log_weights.reshape(groups, LANES), targets)


def per_device(rows, cols, particles, log_weights, targets):
    block = particles.shape[0]
    width = targets.shape[0]
    if rows == 4 and block == 2 * LANES and width % CHUNK == 0 and width % 64 == 0 and width <= 1024:
        return per_device_small(cols, particles, log_weights, targets)
    return per_device_large(particles, log_weights, targets)


def solution(mesh):
    placed = (P("row", None), P("row"), P("col", None))
    return jax.shard_map(
        functools.partial(per_device, mesh.shape["row"], mesh.shape["col"]),
        mesh=mesh,
        in_specs=placed,
        out_specs=P(("col", "row"), None),
        check_vma=False,
    )
```
